32 devices in a mesh: req: 8 (over y, x, core), head: 4 (over z).
Axes of the slice: x: 2, y: 2, z: 4, core: 2. Of those that a mesh axis runs over, the one named last changes fastest.
Arguments:
- queries: bfloat16 [1024, 16384], P(('req', 'head')), may hold values from -15 to 15
- cache_keys: bfloat16 [8, 32768, 1024], P(None, 'req', 'head'), may hold values from -6 to 6
- cache_values: bfloat16 [8, 32768, 1024], P(None, 'req', 'head'), may hold values from -6 to 6
- tree_keys: bfloat16 [1024, 1024], P('req', 'head'), may hold values from -10 to 10
- tree_values: bfloat16 [1024, 1024], P('req', 'head'), may hold values from -6 to 6
- parents: int32 [8, 128], replicated, may hold values from -1 to 126, as said below
- tree_sizes: int32 [8], replicated, may hold values from 16 to 128
- cache_lens: int32 [8], replicated, may hold values from 2 to 32768
Outputs:
- attended: bfloat16 [1024, 16384], P('req', 'head')
The draws below stay inside these ranges and needn't reach their ends.
Inputs may be any that keep to these rules, and one draw needn't show every extreme that they name: parents[a, 0] = -1 (the root); for node i >= 1, parents[a, i] is a node of 0 to i - 1.
All inputs are finite; a program needn't handle non-finite values.
Results may differ from the reference program's by a relative error of at most 0.003.
Values may be sent and summed in bfloat16 or wider, within the bound.
No kernel may reach another device: no remote copies, remote signals or barrier semaphores. Data moves between devices by JAX's collectives and lax.ppermute only.
A program may use at most 192 MiB of HBM per device.

```python
import math
import jax
import jax.numpy as jnp
from jax import lax

NH = 128
KVH = 8
HD = 128
TMAX = 128
REQS = 8
CTX = 32768
ROWS = 1024
N_REQ = 8


def draw_queries(key, part):
    shape = (REQS * TMAX, NH * HD)
    own_key = jax.random.fold_in(key, 11)
    values = 2.5 * jax.random.truncated_normal(own_key, -6.0, 6.0, shape, jnp.float32)
    return values.astype(jnp.bfloat16)


def draw_cache_keys(key, part):
    shape = (REQS, CTX, KVH * HD)
    own_key = jax.random.fold_in(key, 12)
    values = jax.random.truncated_normal(own_key, -6.0, 6.0, shape, jnp.float32)
    return values.astype(jnp.bfloat16)


def draw_parents(key, part):
    node_ids = jnp.arange(TMAX, dtype=jnp.int32)
    jumps = jax.random.randint(jax.random.fold_in(key, 13), (REQS, TMAX), 0, 4, dtype=jnp.int32)
    jumps = jnp.where(node_ids[None, :] == TMAX - 1, 0, jumps)
    reach_back = jnp.minimum(jumps, jnp.maximum(node_ids - 1, 0)[None, :])
    picked = node_ids[None, :] - 1 - reach_back
    return jnp.where(node_ids[None, :] == 0, -1, picked).astype(jnp.int32)


def place_ends(drawn, key, smallest, top_value):
    dims = drawn.shape
    index_at = [jax.random.randint(jax.random.fold_in(key, axis), (), 0, dims[axis]) for axis in range(len(dims))]
    drawn = drawn.at[tuple(index_at)].set(smallest)
    longest = dims.index(max(dims))
    index_at[longest] = (index_at[longest] + 1) % dims[longest]
    return drawn.at[tuple(index_at)].set(top_value)


def steps_of(rng, extent, shards, smallest, top_value):
    level = 1.0
    for axis_at, parts in shards:
        steps = jax.random.uniform(jax.random.fold_in(jax.random.fold_in(rng, 6), axis_at), (parts,), jnp.float32, smallest / len(shards), top_value / len(shards))
        level = level * jnp.repeat(jnp.exp(steps), extent[axis_at] // parts).reshape((-1,) + (1,) * (len(extent) - 1 - axis_at))
    return level


def normal_values(rng, extent, deviation, reach, pieces=(), kind=jnp.bfloat16):
    values = deviation * jax.random.normal(rng, extent, jnp.float32)
    if pieces:
        values = values * steps_of(rng, extent, pieces, -0.22, 0.18)
    return jnp.clip(values, -reach, reach).astype(kind)


def setup_inputs(seed: int = 0) -> dict:
    seeds = jax.random.split(jax.random.key(seed), 9)
    return {
        "queries": draw_queries(jax.random.fold_in(seeds[8], 71), 0),
        "cache_keys": draw_cache_keys(jax.random.fold_in(seeds[8], 71), 0),
        "cache_values": normal_values(seeds[2], (REQS, CTX, KVH * HD), 1.0, 6.0, ((1, 8), (2, 4))),
        "tree_keys": normal_values(seeds[3], (ROWS, KVH * HD), 1.7, 10.0, ((0, 8), (1, 4))),
        "tree_values": normal_values(seeds[4], (ROWS, KVH * HD), 1.0, 6.0, ((0, 8), (1, 4))),
        "parents": draw_parents(jax.random.fold_in(seeds[8], 71), 0),
        "tree_sizes": place_ends(jax.random.randint(seeds[6], (REQS,), 16, TMAX + 1), jax.random.fold_in(seeds[6], 1), 16, TMAX).astype(jnp.int32),
        "cache_lens": place_ends(jax.random.randint(seeds[7], (REQS,), 2, CTX + 1), jax.random.fold_in(seeds[7], 1), 2, CTX).astype(jnp.int32),
    }


negative_fill = -1e+30

def ancestry(parents):
    node_ids = jnp.arange(TMAX, dtype=jnp.int32)
    linked = jnp.logical_or(parents[:, :, None] == node_ids[None, None, :], node_ids[:, None] == node_ids[None, :])
    reached = linked.astype(jnp.float32)
    for doubling in range((TMAX - 1).bit_length()):
        squared = jnp.einsum('aij,ajk->aik', reached, reached, precision=lax.Precision.HIGHEST)
        reached = jnp.minimum(squared, 1.0)
    return reached

def reference(queries, cache_keys, cache_values, tree_keys, tree_values, parents, tree_sizes, cache_lens):
    group_size = NH // KVH
    softmax_scale = 1.0 / math.sqrt(HD)
    cache_block = CTX // N_REQ
    rows_owned = REQS * TMAX // N_REQ
    reached = ancestry(parents)
    owners = jnp.arange(N_REQ, dtype=jnp.int32)
    node_ids = jnp.arange(TMAX, dtype=jnp.int32)
    positions = jnp.arange(CTX, dtype=jnp.int32).reshape(N_REQ, cache_block)

    def one_request(request):
        start = request * TMAX
        query_block = lax.dynamic_slice_in_dim(queries, start, TMAX, 0).astype(jnp.float32)
        query_block = query_block.reshape(TMAX, KVH, group_size, HD).transpose(1, 0, 2, 3)
        block_keys = lax.dynamic_index_in_dim(cache_keys, request, 0, keepdims=False).astype(jnp.float32)
        block_keys = block_keys.reshape(N_REQ, cache_block, KVH, HD).transpose(2, 0, 1, 3)
        block_values = lax.dynamic_index_in_dim(cache_values, request, 0, keepdims=False).astype(jnp.float32)
        block_values = block_values.reshape(N_REQ, cache_block, KVH, HD).transpose(2, 0, 1, 3)
        node_keys = lax.dynamic_slice_in_dim(tree_keys, start, TMAX, 0).astype(jnp.float32)
        node_keys = node_keys.reshape(TMAX, KVH, HD).transpose(1, 0, 2)
        node_values = lax.dynamic_slice_in_dim(tree_values, start, TMAX, 0).astype(jnp.float32)
        node_values = node_values.reshape(TMAX, KVH, HD).transpose(1, 0, 2)
        length = lax.dynamic_index_in_dim(cache_lens, request, 0, keepdims=False)
        live_cache = positions < length
        live_tree = lax.dynamic_index_in_dim(reached, request, 0, keepdims=False) > 0.5
        member = ((start + node_ids) // rows_owned)[:, None] == owners[None, :]

        def one_head(operands):
            head_queries, head_keys, head_values, head_nodes, head_node_values = operands
            cache_scores = jnp.einsum('iqd,jpd->iqjp', head_queries, head_keys, precision=lax.Precision.HIGHEST) * softmax_scale
            cache_scores = jnp.where(live_cache[None, None], cache_scores, negative_fill)
            tree_scores = jnp.einsum('iqd,kd->iqk', head_queries, head_nodes, precision=lax.Precision.HIGHEST) * softmax_scale
            tree_scores = jnp.where(live_tree[:, None, :], tree_scores, negative_fill)
            grouped = jnp.where(member[None, None], tree_scores[..., None], negative_fill)
            peaks = jnp.maximum(lax.optimization_barrier(jnp.max(cache_scores, axis=3)), lax.optimization_barrier(jnp.max(grouped, axis=2)))
            cache_weights = jnp.where(live_cache[None, None], jnp.exp(cache_scores - peaks[..., None]), 0.0)
            tree_live = jnp.logical_and(live_tree[:, None, :, None], member[None, None])
            tree_weights = jnp.where(tree_live, jnp.exp(grouped - peaks[:, :, None, :]), 0.0)
            totals = lax.optimization_barrier(jnp.sum(cache_weights, axis=3)) + lax.optimization_barrier(jnp.sum(tree_weights, axis=2))
            cache_rounded = lax.optimization_barrier(cache_weights.astype(jnp.bfloat16)).astype(jnp.float32)
            tree_rounded = lax.optimization_barrier(tree_weights.astype(jnp.bfloat16)).astype(jnp.float32)
            group_sums = jnp.einsum('iqjp,jpd->iqjd', cache_rounded, head_values, precision=lax.Precision.HIGHEST)
            group_sums = group_sums + jnp.einsum('iqkj,kd->iqjd', tree_rounded, head_node_values, precision=lax.Precision.HIGHEST)
            floored = jnp.maximum(totals, 1.0)
            partials = group_sums / floored[..., None]
            log_totals = peaks + jnp.log(floored)
            highest = lax.optimization_barrier(jnp.max(log_totals, axis=2))
            weights = jnp.exp(log_totals - highest[..., None])
            return lax.optimization_barrier(jnp.sum(weights[..., None] * partials, axis=2)) / lax.optimization_barrier(jnp.sum(weights, axis=2))[..., None]
        merged = lax.map(one_head, (query_block, block_keys, block_values, node_keys, node_values))
        merged = merged.transpose(1, 0, 2, 3).reshape(TMAX, NH * HD)
        live_size = lax.dynamic_index_in_dim(tree_sizes, request, 0, keepdims=False)
        return jnp.where((node_ids < live_size)[:, None], merged, 0.0).astype(jnp.bfloat16)
    attended = lax.map(one_request, jnp.arange(REQS, dtype=jnp.int32))
    return attended.reshape(REQS * TMAX, NH * HD)
```

```python
import functools
import math

import jax
import jax.numpy as jnp
from jax import lax
from jax.experimental import pallas as pl
from jax.experimental.pallas import tpu as pltpu
from jax.sharding import PartitionSpec as P

NH = 128
KVH = 8
HD = 128
GROUP = NH // KVH
LANES = 128

negative_fill = -1e30
softmax_scale = 1.0 / math.sqrt(HD)
exp2_scale = softmax_scale * math.log2(math.e)
wire = jnp.bfloat16


def lane_max(scores):
    best = scores[:, :LANES]
    for at in range(LANES, scores.shape[1], LANES):
        best = jnp.maximum(best, scores[:, at : at + LANES])
    return best


def place_logs(logs, nodes, first_head):
    lane = lax.broadcasted_iota(jnp.int32, (nodes, LANES), 1)
    placed = jnp.full((nodes, LANES), 0.0, jnp.float32)
    for head in range(GROUP):
        placed = jnp.where(lane == first_head + head, logs[head * nodes : (head + 1) * nodes, :], placed)
    mask = jnp.logical_and(lane >= first_head, lane < first_head + GROUP)
    return placed, mask


def cache_kernel(
    chunk, lens_ref, sizes_ref, base_ref, q_ref, k_ref, v_ref, o_ref, l_ref, s_ref, x_ref, a_ref
):
    request = pl.program_id(0)
    kv_head = pl.program_id(1)
    block = k_ref.shape[1]
    live = jnp.clip(lens_ref[request] - base_ref[0], 0, block)
    size = sizes_ref[request]
    full_chunks = live // chunk
    rest = live - full_chunks * chunk
    first_head = kv_head * GROUP

    def tile(start, nodes):
        rows = GROUP * nodes
        queries = jnp.concatenate(
            [q_ref[pl.ds(start, nodes), h * HD : (h + 1) * HD] for h in range(GROUP)], axis=0
        )

        def score(at):
            return lax.dot_general(
                queries,
                k_ref[0, pl.ds(at, chunk), :],
                (((1,), (1,)), ((), ())),
                preferred_element_type=jnp.float32,
            )

        a_ref[:rows, :LANES] = jnp.full((rows, LANES), negative_fill, jnp.float32)

        @pl.loop(0, full_chunks)
        def _(c):
            at = pl.multiple_of(c * chunk, chunk)
            scores = score(at)
            s_ref[:rows, pl.ds(at, chunk)] = scores
            a_ref[:rows, :LANES] = jnp.maximum(a_ref[:rows, :LANES], lane_max(scores))

        @pl.when(rest > 0)
        def _():
            at = pl.multiple_of(full_chunks * chunk, chunk)
            column = lax.broadcasted_iota(jnp.int32, (rows, chunk), 1)
            scores = jnp.where(column < rest, score(at), negative_fill)
            s_ref[:rows, pl.ds(at, chunk)] = scores
            a_ref[:rows, :LANES] = jnp.maximum(a_ref[:rows, :LANES], lane_max(scores))

        peaks = jnp.max(a_ref[:rows, :LANES], axis=1, keepdims=True)
        shift = peaks * exp2_scale
        a_ref[:rows, :] = jnp.zeros((rows, 2 * LANES), jnp.float32)

        @pl.loop(0, full_chunks + (rest > 0).astype(jnp.int32))
        def _(c):
            at = pl.multiple_of(c * chunk, chunk)
            weights = jnp.exp2(s_ref[:rows, pl.ds(at, chunk)] * exp2_scale - shift).astype(jnp.bfloat16)
            a_ref[:rows, :] += jnp.dot(
                weights, x_ref[pl.ds(at, chunk), :], preferred_element_type=jnp.float32
            )

        totals = jnp.maximum(a_ref[:rows, LANES:], 1.0)
        partials = (a_ref[:rows, :LANES] / totals).astype(o_ref.dtype)
        for h in range(GROUP):
            o_ref[pl.ds(start, nodes), h * HD : (h + 1) * HD] = partials[h * nodes : (h + 1) * nodes, :]
        placed, mask = place_logs(peaks * softmax_scale + jnp.log(totals), nodes, first_head)
        l_ref[pl.ds(start, nodes), :] = jnp.where(mask, placed, l_ref[pl.ds(start, nodes), :])

    @pl.when(kv_head == 0)
    def _():
        l_ref[...] = jnp.full(l_ref.shape, negative_fill, jnp.float32)

    @pl.when(live == 0)
    def _():
        o_ref[...] = jnp.zeros(o_ref.shape, o_ref.dtype)

    @pl.when(live > 0)
    def _():
        x_ref[:, :HD] = v_ref[0]
        x_ref[:, HD:] = jnp.ones((block, LANES), x_ref.dtype)
        wide = size // 32
        left = size - wide * 32

        @pl.loop(0, wide + (left > 16).astype(jnp.int32))
        def _(t):
            tile(pl.multiple_of(t * 32, 32), 32)

        @pl.when(jnp.logical_and(left > 0, left <= 16))
        def _():
            tile(pl.multiple_of(wide * 32, 32), 16)


def cache_attention(queries, cache_keys, cache_values, lens, sizes, base, node_count):
    requests, block, width = cache_keys.shape
    kv_local = width // HD
    rows, columns = queries.shape
    chunk = min(block, 1024)
    grid_spec = pltpu.PrefetchScalarGridSpec(
        num_scalar_prefetch=3,
        grid=(requests, kv_local),
        in_specs=[
            pl.BlockSpec((node_count, GROUP * HD), lambda b, g, *_: (b, g)),
            pl.BlockSpec((1, block, HD), lambda b, g, *_: (b, 0, g)),
            pl.BlockSpec((1, block, HD), lambda b, g, *_: (b, 0, g)),
        ],
        out_specs=[
            pl.BlockSpec((node_count, GROUP * HD), lambda b, g, *_: (b, g)),
            pl.BlockSpec((node_count, LANES), lambda b, g, *_: (b, 0)),
        ],
        scratch_shapes=[
            pltpu.VMEM((32 * GROUP, block), jnp.float32),
            pltpu.VMEM((block, 2 * LANES), jnp.bfloat16),
            pltpu.VMEM((32 * GROUP, 2 * LANES), jnp.float32),
        ],
    )
    return pl.pallas_call(
        functools.partial(cache_kernel, chunk),
        grid_spec=grid_spec,
        out_shape=[
            jax.ShapeDtypeStruct((rows, columns), wire),
            jax.ShapeDtypeStruct((rows, LANES), jnp.float32),
        ],
        compiler_params=pltpu.CompilerParams(vmem_limit_bytes=48 * 1024 * 1024),
        cost_estimate=pl.CostEstimate(
            flops=2 * rows * (columns // HD) * block * HD * 2,
            bytes_accessed=4 * cache_keys.size + 4 * queries.size,
            transcendentals=rows * (columns // HD) * block,
        ),
    )(lens, sizes, base, queries, cache_keys, cache_values)


def tree_kernel(first_ref, q_ref, k_ref, v_ref, parents_ref, o_ref, l_ref, r_ref):
    rows_owned = q_ref.shape[0]
    node_count = k_ref.shape[0]
    kv_local = k_ref.shape[1] // HD
    steps = (node_count - 1).bit_length()
    node = lax.broadcasted_iota(jnp.int32, (node_count, node_count), 0)
    other = lax.broadcasted_iota(jnp.int32, (node_count, node_count), 1)
    linked = jnp.logical_or(parents_ref[...] == node, node == other)
    reached = linked.astype(jnp.float32)
    for _ in range(steps):
        half = reached.astype(jnp.bfloat16)
        reached = jnp.minimum(jnp.dot(half, half, preferred_element_type=jnp.float32), 1.0)
    r_ref[...] = reached.T
    tile = min(rows_owned, 32)
    l_ref[...] = jnp.full(l_ref.shape, negative_fill, jnp.float32)
    for g in range(kv_local):
        keys = k_ref[:, g * HD : (g + 1) * HD]
        values = v_ref[:, g * HD : (g + 1) * HD]

        @pl.loop(0, rows_owned // tile)
        def _(t):
            start = pl.multiple_of(t * tile, tile)
            first = pl.multiple_of(first_ref[0] + start, tile)
            columns = g * GROUP * HD
            queries = jnp.concatenate(
                [
                    q_ref[pl.ds(start, tile), columns + h * HD : columns + (h + 1) * HD]
                    for h in range(GROUP)
                ],
                axis=0,
            )
            live = jnp.concatenate([r_ref[pl.ds(first, tile), :]] * GROUP, axis=0) > 0.5
            scores = lax.dot_general(
                queries, keys, (((1,), (1,)), ((), ())), preferred_element_type=jnp.float32
            )
            scores = jnp.where(live, scores, negative_fill)
            peaks = jnp.max(scores, axis=1, keepdims=True)
            weights = jnp.where(live, jnp.exp2((scores - peaks) * exp2_scale), 0.0)
            totals = jnp.maximum(jnp.sum(weights, axis=1, keepdims=True), 1.0)
            sums = jnp.dot(weights.astype(jnp.bfloat16), values, preferred_element_type=jnp.float32)
            partials = (sums / totals).astype(o_ref.dtype)
            for h in range(GROUP):
                o_ref[pl.ds(start, tile), columns + h * HD : columns + (h + 1) * HD] = partials[
                    h * tile : (h + 1) * tile, :
                ]
            logs = jnp.broadcast_to(peaks * softmax_scale + jnp.log(totals), (GROUP * tile, LANES))
            placed, mask = place_logs(logs, tile, g * GROUP)
            l_ref[pl.ds(start, tile), :] = jnp.where(mask, placed, l_ref[pl.ds(start, tile), :])


def tree_attention(queries, keys, values, parents, first):
    rows, columns = queries.shape
    node_count = keys.shape[0]
    vmem = pl.BlockSpec(memory_space=pltpu.VMEM)
    return pl.pallas_call(
        tree_kernel,
        in_specs=[pl.BlockSpec(memory_space=pltpu.SMEM)] + [vmem] * 4,
        out_specs=[vmem, vmem],
        out_shape=[
            jax.ShapeDtypeStruct((rows, columns), jnp.float32),
            jax.ShapeDtypeStruct((rows, LANES), jnp.float32),
        ],
        scratch_shapes=[pltpu.VMEM((node_count, node_count), jnp.float32)],
        compiler_params=pltpu.CompilerParams(vmem_limit_bytes=32 * 1024 * 1024),
    )(first, queries, keys, values, parents)


def merge_kernel(p_ref, l_ref, tree_ref, tree_logs_ref, alive_ref, o_ref):
    parts = p_ref.shape[0]
    logs = [l_ref[j] for j in range(parts)] + [tree_logs_ref[...]]
    top = functools.reduce(jnp.maximum, logs)
    weights = [jnp.exp(log - top) for log in logs]
    scale = alive_ref[...] / functools.reduce(jnp.add, weights)
    shares = [weight * scale for weight in weights]
    heads = p_ref.shape[2] // HD
    lane0 = pl.program_id(0) * heads
    for h in range(heads):
        at = slice(h * HD, (h + 1) * HD)
        total = None
        for j in range(parts + 1):
            piece = tree_ref[:, at] if j == parts else p_ref[j, :, at].astype(jnp.float32)
            term = piece * shares[j][:, h : h + 1]
            total = term if total is None else total + term
        o_ref[:, at] = jnp.where(alive_ref[...] > 0.5, total, 0.0).astype(o_ref.dtype)


def merge(partials, logs, tree_partials, tree_logs, alive):
    parts, rows, columns = partials.shape
    return pl.pallas_call(
        merge_kernel,
        grid=(1,),
        in_specs=[
            pl.BlockSpec((parts, rows, columns), lambda i: (0, 0, 0)),
            pl.BlockSpec((parts, rows, LANES), lambda i: (0, 0, 0)),
            pl.BlockSpec((rows, columns), lambda i: (0, 0)),
            pl.BlockSpec((rows, LANES), lambda i: (0, 0)),
            pl.BlockSpec((rows, LANES), lambda i: (0, 0)),
        ],
        out_specs=pl.BlockSpec((rows, columns), lambda i: (0, 0)),
        out_shape=jax.ShapeDtypeStruct((rows, columns), jnp.bfloat16),
        compiler_params=pltpu.CompilerParams(vmem_limit_bytes=56 * 1024 * 1024),
    )(partials, logs, tree_partials, tree_logs, alive)


def body(
    queries, cache_keys, cache_values, tree_keys, tree_values, parents, tree_sizes, cache_lens
):
    owner_index = lax.axis_index("req")
    owners = lax.axis_size("req")
    block = cache_keys.shape[1]
    node_count = parents.shape[1]
    rows_owned = tree_keys.shape[0]
    by_head = lax.all_to_all(queries, "head", split_axis=1, concat_axis=0, tiled=True)
    all_rows = lax.all_gather(by_head, "req", axis=0, tiled=True)

    first_row = owner_index * rows_owned
    request = first_row // node_count
    first_node = first_row % node_count
    if rows_owned < node_count:
        every_key = lax.all_gather(tree_keys, "req", axis=0, tiled=True)
        every_value = lax.all_gather(tree_values, "req", axis=0, tiled=True)
        own_keys = lax.dynamic_slice_in_dim(every_key, request * node_count, node_count, 0)
        own_values = lax.dynamic_slice_in_dim(every_value, request * node_count, node_count, 0)
    else:
        own_keys, own_values = tree_keys, tree_values
    own_parents = lax.dynamic_slice_in_dim(parents, request, 1, 0)
    tree_partials, tree_logs = tree_attention(
        by_head, own_keys, own_values, own_parents, first_node[None]
    )

    base = (owner_index * block)[None]
    partials, logs = cache_attention(
        all_rows, cache_keys, cache_values, cache_lens, tree_sizes, base, node_count
    )
    columns = partials.shape[1]
    partials = lax.all_to_all(
        partials.reshape(owners, rows_owned, columns), "req", split_axis=0, concat_axis=0
    )
    logs = lax.all_to_all(
        logs.reshape(owners, rows_owned, LANES), "req", split_axis=0, concat_axis=0
    )
    size = lax.dynamic_index_in_dim(tree_sizes, request, 0, keepdims=False)
    alive = first_node + jnp.arange(rows_owned, dtype=jnp.int32) < size
    alive = jnp.broadcast_to(alive[:, None].astype(jnp.float32), (rows_owned, LANES))
    return merge(partials, logs, tree_partials, tree_logs, alive)


def solution(mesh):
    placed = (
        P(("req", "head"), None),
        P(None, "req", "head"),
        P(None, "req", "head"),
        P("req", "head"),
        P("req", "head"),
        P(),
        P(),
        P(),
    )
    return jax.shard_map(
        body, mesh=mesh, in_specs=placed, out_specs=P("req", "head"), check_vma=False
    )
```

```python
import functools
import math

import jax
import jax.numpy as jnp
from jax import lax
from jax.experimental import pallas as pl
from jax.experimental.pallas import tpu as pltpu
from jax.sharding import PartitionSpec as P

NH = 128
KVH = 8
HD = 128
GROUP = NH // KVH
LANES = 128

negative_fill = -1e30
softmax_scale = 1.0 / math.sqrt(HD)
exp2_scale = softmax_scale * math.log2(math.e)
wire = jnp.bfloat16


def lane_max(scores):
    best = scores[:, :LANES]
    for at in range(LANES, scores.shape[1], LANES):
        best = jnp.maximum(best, scores[:, at : at + LANES])
    return best


def place_logs(logs, nodes, first_head):
    lane = lax.broadcasted_iota(jnp.int32, (nodes, LANES), 1)
    placed = jnp.full((nodes, LANES), 0.0, jnp.float32)
    for head in range(GROUP):
        placed = jnp.where(lane == first_head + head, logs[head * nodes : (head + 1) * nodes, :], placed)
    mask = jnp.logical_and(lane >= first_head, lane < first_head + GROUP)
    return placed, mask


def cache_kernel(
    chunk, lens_ref, sizes_ref, base_ref, q_ref, k_ref, v_ref, o_ref, l_ref, p_ref, x_ref, a_ref, t_ref, h_ref
):
    request = pl.program_id(0)
    kv_head = pl.program_id(1)
    block = k_ref.shape[1]
    live = jnp.clip(lens_ref[request] - base_ref[0], 0, block)
    size = sizes_ref[request]
    first_head = kv_head * GROUP
    step = 256
    part = min(block, 512)
    part_chunks = (live + part - 1) // part

    def score(rows, at, width):
        return lax.dot_general(
            t_ref[:rows, :],
            k_ref[0, pl.ds(at, width), :],
            (((1,), (1,)), ((), ())),
            preferred_element_type=jnp.float32,
        )

    def weigh(scores, rows):
        shift = h_ref[:rows, :]
        return [
            jnp.exp2(scores[:, i : i + LANES] * exp2_scale - shift)
            for i in range(0, scores.shape[1], LANES)
        ]

    def masked(scores, at):
        column = lax.broadcasted_iota(jnp.int32, scores.shape, 1)
        return jnp.where(column < live - at, scores, negative_fill)

    def set_shift(best):
        peaks = jnp.max(best, axis=1, keepdims=True) * exp2_scale
        h_ref[: best.shape[0], :] = jnp.broadcast_to(peaks, best.shape)

    def whole_block(rows):
        for c in range(0, block, chunk):
            for at in range(c, c + chunk, step):
                pieces = weigh(score(rows, at, step), rows)
                for i, piece in enumerate(pieces):
                    p_ref[:rows, at + i * LANES : at + (i + 1) * LANES] = piece.astype(jnp.bfloat16)
            sums = jnp.dot(
                p_ref[:rows, c : c + chunk], x_ref[c : c + chunk, :], preferred_element_type=jnp.float32
            )
            a_ref[:rows, :] = sums if c == 0 else a_ref[:rows, :] + sums

    def part_block(rows):
        a_ref[:rows, :] = jnp.zeros((rows, 2 * LANES), jnp.float32)

        @pl.loop(0, part_chunks)
        def _(c):
            at = pl.multiple_of(c * part, part)
            pieces = weigh(masked(score(rows, at, part), at), rows)
            weights = jnp.concatenate([piece.astype(jnp.bfloat16) for piece in pieces], axis=1)
            a_ref[:rows, :] += jnp.dot(
                weights, x_ref[pl.ds(at, part), :], preferred_element_type=jnp.float32
            )

    def tile(start, nodes):
        rows = GROUP * nodes
        for h in range(GROUP):
            t_ref[h * nodes : (h + 1) * nodes, :] = q_ref[pl.ds(start, nodes), h * HD : (h + 1) * HD]
        set_shift(masked(score(rows, 0, LANES), 0))

        @pl.when(live == block)
        def _():
            whole_block(rows)

        @pl.when(live < block)
        def _():
            part_block(rows)

        fits = jnp.max(a_ref[:rows, LANES:]) < 2.0**100

        @pl.when(jnp.logical_not(fits))
        def _():
            a_ref[:rows, :LANES] = jnp.full((rows, LANES), negative_fill, jnp.float32)

            @pl.loop(0, part_chunks)
            def _(c):
                at = pl.multiple_of(c * part, part)
                best = lane_max(masked(score(rows, at, part), at))
                a_ref[:rows, :LANES] = jnp.maximum(a_ref[:rows, :LANES], best)

            set_shift(a_ref[:rows, :LANES])
            part_block(rows)

        totals = a_ref[:rows, LANES:]
        partials = (a_ref[:rows, :LANES] / totals).astype(o_ref.dtype)
        for h in range(GROUP):
            o_ref[pl.ds(start, nodes), h * HD : (h + 1) * HD] = partials[h * nodes : (h + 1) * nodes, :]
        logs = h_ref[:rows, :] * math.log(2.0) + jnp.log(totals)
        placed, mask = place_logs(logs, nodes, first_head)
        l_ref[pl.ds(start, nodes), :] = jnp.where(mask, placed, l_ref[pl.ds(start, nodes), :])

    @pl.when(kv_head == 0)
    def _():
        l_ref[...] = jnp.full(l_ref.shape, negative_fill, jnp.float32)

    @pl.when(jnp.logical_and(request == 0, kv_head == 0))
    def _():
        x_ref[:, HD:] = jnp.ones((block, LANES), x_ref.dtype)

    @pl.when(live == 0)
    def _():
        o_ref[...] = jnp.zeros(o_ref.shape, o_ref.dtype)

    @pl.when(live > 0)
    def _():
        x_ref[:, :HD] = v_ref[0]
        wide = size // 32
        left = size - wide * 32

        @pl.loop(0, wide + (left > 16).astype(jnp.int32))
        def _(t):
            tile(pl.multiple_of(t * 32, 32), 32)

        @pl.when(jnp.logical_and(left > 0, left <= 16))
        def _():
            tile(pl.multiple_of(wide * 32, 32), 16)


def cache_attention(queries, cache_keys, cache_values, lens, sizes, base, node_count):
    requests, block, width = cache_keys.shape
    kv_local = width // HD
    rows, columns = queries.shape
    chunk = min(block, 1024)
    grid_spec = pltpu.PrefetchScalarGridSpec(
        num_scalar_prefetch=3,
        grid=(requests, kv_local),
        in_specs=[
            pl.BlockSpec((node_count, GROUP * HD), lambda b, g, *_: (b, g)),
            pl.BlockSpec((1, block, HD), lambda b, g, *_: (b, 0, g)),
            pl.BlockSpec((1, block, HD), lambda b, g, *_: (b, 0, g)),
        ],
        out_specs=[
            pl.BlockSpec((node_count, GROUP * HD), lambda b, g, *_: (b, g)),
            pl.BlockSpec((node_count, LANES), lambda b, g, *_: (b, 0)),
        ],
        scratch_shapes=[
            pltpu.VMEM((32 * GROUP, block), jnp.bfloat16),
            pltpu.VMEM((block, 2 * LANES), jnp.bfloat16),
            pltpu.VMEM((32 * GROUP, 2 * LANES), jnp.float32),
            pltpu.VMEM((32 * GROUP, HD), jnp.bfloat16),
            pltpu.VMEM((32 * GROUP, LANES), jnp.float32),
        ],
    )
    return pl.pallas_call(
        functools.partial(cache_kernel, chunk),
        grid_spec=grid_spec,
        out_shape=[
            jax.ShapeDtypeStruct((rows, columns), wire),
            jax.ShapeDtypeStruct((rows, LANES), jnp.float32),
        ],
        compiler_params=pltpu.CompilerParams(vmem_limit_bytes=48 * 1024 * 1024),
        cost_estimate=pl.CostEstimate(
            flops=2 * rows * (columns // HD) * block * HD * 2,
            bytes_accessed=4 * cache_keys.size + 4 * queries.size,
            transcendentals=rows * (columns // HD) * block,
        ),
    )(lens, sizes, base, queries, cache_keys, cache_values)


def tree_kernel(first_ref, q_ref, k_ref, v_ref, parents_ref, o_ref, l_ref, r_ref):
    rows_owned = q_ref.shape[0]
    node_count = k_ref.shape[0]
    kv_local = k_ref.shape[1] // HD
    steps = (node_count - 1).bit_length()
    node = lax.broadcasted_iota(jnp.int32, (node_count, node_count), 0)
    other = lax.broadcasted_iota(jnp.int32, (node_count, node_count), 1)
    linked = jnp.logical_or(parents_ref[...] == node, node == other)
    reached = linked.astype(jnp.float32)
    for _ in range(steps):
        half = reached.astype(jnp.bfloat16)
        reached = jnp.minimum(jnp.dot(half, half, preferred_element_type=jnp.float32), 1.0)
    r_ref[...] = reached.T
    tile = min(rows_owned, 32)
    l_ref[...] = jnp.full(l_ref.shape, negative_fill, jnp.float32)
    for g in range(kv_local):
        keys = k_ref[:, g * HD : (g + 1) * HD]
        values = v_ref[:, g * HD : (g + 1) * HD]

        @pl.loop(0, rows_owned // tile)
        def _(t):
            start = pl.multiple_of(t * tile, tile)
            first = pl.multiple_of(first_ref[0] + start, tile)
            columns = g * GROUP * HD
            queries = jnp.concatenate(
                [
                    q_ref[pl.ds(start, tile), columns + h * HD : columns + (h + 1) * HD]
                    for h in range(GROUP)
                ],
                axis=0,
            )
            live = jnp.concatenate([r_ref[pl.ds(first, tile), :]] * GROUP, axis=0) > 0.5
            scores = lax.dot_general(
                queries, keys, (((1,), (1,)), ((), ())), preferred_element_type=jnp.float32
            )
            scores = jnp.where(live, scores, negative_fill)
            peaks = jnp.max(scores, axis=1, keepdims=True)
            weights = jnp.where(live, jnp.exp2((scores - peaks) * exp2_scale), 0.0)
            totals = jnp.maximum(jnp.sum(weights, axis=1, keepdims=True), 1.0)
            sums = jnp.dot(weights.astype(jnp.bfloat16), values, preferred_element_type=jnp.float32)
            partials = (sums / totals).astype(o_ref.dtype)
            for h in range(GROUP):
                o_ref[pl.ds(start, tile), columns + h * HD : columns + (h + 1) * HD] = partials[
                    h * tile : (h + 1) * tile, :
                ]
            logs = jnp.broadcast_to(peaks * softmax_scale + jnp.log(totals), (GROUP * tile, LANES))
            placed, mask = place_logs(logs, tile, g * GROUP)
            l_ref[pl.ds(start, tile), :] = jnp.where(mask, placed, l_ref[pl.ds(start, tile), :])


def tree_attention(queries, keys, values, parents, first):
    rows, columns = queries.shape
    node_count = keys.shape[0]
    vmem = pl.BlockSpec(memory_space=pltpu.VMEM)
    return pl.pallas_call(
        tree_kernel,
        in_specs=[pl.BlockSpec(memory_space=pltpu.SMEM)] + [vmem] * 4,
        out_specs=[vmem, vmem],
        out_shape=[
            jax.ShapeDtypeStruct((rows, columns), jnp.float32),
            jax.ShapeDtypeStruct((rows, LANES), jnp.float32),
        ],
        scratch_shapes=[pltpu.VMEM((node_count, node_count), jnp.float32)],
        compiler_params=pltpu.CompilerParams(vmem_limit_bytes=32 * 1024 * 1024),
    )(first, queries, keys, values, parents)


def merge_kernel(p_ref, l_ref, tree_ref, tree_logs_ref, alive_ref, o_ref):
    parts = p_ref.shape[0]
    logs = [l_ref[j] for j in range(parts)] + [tree_logs_ref[...]]
    top = functools.reduce(jnp.maximum, logs)
    weights = [jnp.exp(log - top) for log in logs]
    scale = alive_ref[...] / functools.reduce(jnp.add, weights)
    shares = [weight * scale for weight in weights]
    heads = p_ref.shape[2] // HD
    lane0 = pl.program_id(0) * heads
    for h in range(heads):
        at = slice(h * HD, (h + 1) * HD)
        total = None
        for j in range(parts + 1):
            piece = tree_ref[:, at] if j == parts else p_ref[j, :, at].astype(jnp.float32)
            term = piece * shares[j][:, h : h + 1]
            total = term if total is None else total + term
        o_ref[:, at] = jnp.where(alive_ref[...] > 0.5, total, 0.0).astype(o_ref.dtype)


def merge(partials, logs, tree_partials, tree_logs, alive):
    parts, rows, columns = partials.shape
    return pl.pallas_call(
        merge_kernel,
        grid=(1,),
        in_specs=[
            pl.BlockSpec((parts, rows, columns), lambda i: (0, 0, 0)),
            pl.BlockSpec((parts, rows, LANES), lambda i: (0, 0, 0)),
            pl.BlockSpec((rows, columns), lambda i: (0, 0)),
            pl.BlockSpec((rows, LANES), lambda i: (0, 0)),
            pl.BlockSpec((rows, LANES), lambda i: (0, 0)),
        ],
        out_specs=pl.BlockSpec((rows, columns), lambda i: (0, 0)),
        out_shape=jax.ShapeDtypeStruct((rows, columns), jnp.bfloat16),
        compiler_params=pltpu.CompilerParams(vmem_limit_bytes=56 * 1024 * 1024),
    )(partials, logs, tree_partials, tree_logs, alive)


def body(
    queries, cache_keys, cache_values, tree_keys, tree_values, parents, tree_sizes, cache_lens
):
    owner_index = lax.axis_index("req")
    owners = lax.axis_size("req")
    block = cache_keys.shape[1]
    node_count = parents.shape[1]
    rows_owned = tree_keys.shape[0]
    by_head = lax.all_to_all(queries, "head", split_axis=1, concat_axis=0, tiled=True)
    all_rows = lax.all_gather(by_head, "req", axis=0, tiled=True)

    first_row = owner_index * rows_owned
    request = first_row // node_count
    first_node = first_row % node_count
    if rows_owned < node_count:
        every_key = lax.all_gather(tree_keys, "req", axis=0, tiled=True)
        every_value = lax.all_gather(tree_values, "req", axis=0, tiled=True)
        own_keys = lax.dynamic_slice_in_dim(every_key, request * node_count, node_count, 0)
        own_values = lax.dynamic_slice_in_dim(every_value, request * node_count, node_count, 0)
    else:
        own_keys, own_values = tree_keys, tree_values
    own_parents = lax.dynamic_slice_in_dim(parents, request, 1, 0)
    tree_partials, tree_logs = tree_attention(
        by_head, own_keys, own_values, own_parents, first_node[None]
    )

    base = (owner_index * block)[None]
    partials, logs = cache_attention(
        all_rows, cache_keys, cache_values, cache_lens, tree_sizes, base, node_count
    )
    columns = partials.shape[1]
    partials = lax.all_to_all(
        partials.reshape(owners, rows_owned, columns), "req", split_axis=0, concat_axis=0
    )
    logs = lax.all_to_all(
        logs.reshape(owners, rows_owned, LANES), "req", split_axis=0, concat_axis=0
    )
    size = lax.dynamic_index_in_dim(tree_sizes, request, 0, keepdims=False)
    alive = first_node + jnp.arange(rows_owned, dtype=jnp.int32) < size
    alive = jnp.broadcast_to(alive[:, None].astype(jnp.float32), (rows_owned, LANES))
    return merge(partials, logs, tree_partials, tree_logs, alive)


def solution(mesh):
    placed = (
        P(("req", "head"), None),
        P(None, "req", "head"),
        P(None, "req", "head"),
        P("req", "head"),
        P("req", "head"),
        P(),
        P(),
        P(),
    )
    return jax.shard_map(
        body, mesh=mesh, in_specs=placed, out_specs=P("req", "head"), check_vma=False
    )
```

```python
import functools
import math

import jax
import jax.numpy as jnp
from jax import lax
from jax.experimental import pallas as pl
from jax.experimental.pallas import tpu as pltpu
from jax.sharding import PartitionSpec as P

NH = 128
KVH = 8
HD = 128
GROUP = NH // KVH
WIDE = GROUP * HD
LANES = 128
NODES = 32
ROWS = GROUP * NODES

negative_fill = -1e30
softmax_scale = 1.0 / math.sqrt(HD)
exp2_scale = softmax_scale * math.log2(math.e)
wire = jnp.bfloat16


def lane_max(scores):
    best = scores[:, :LANES]
    for at in range(LANES, scores.shape[1], LANES):
        best = jnp.maximum(best, scores[:, at : at + LANES])
    return best


def place_logs(logs):
    lane = lax.broadcasted_iota(jnp.int32, logs[0].shape, 1) % GROUP
    placed = logs[0]
    for head in range(1, GROUP):
        placed = jnp.where(lane == head, logs[head], placed)
    return placed


def split_logs(logs):
    high = logs.astype(wire).astype(jnp.float32)
    rest = logs - high
    middle = rest.astype(wire).astype(jnp.float32)
    group = lax.broadcasted_iota(jnp.int32, logs.shape, 1) // GROUP
    parts = jnp.where(group == 0, high, jnp.where(group == 1, middle, rest - middle))
    return parts.astype(wire)


def join_logs(parts):
    parts = parts.astype(jnp.float32)
    return parts + pltpu.roll(parts, LANES - GROUP, 1) + pltpu.roll(parts, LANES - 2 * GROUP, 1)


def unit_kernel(units, merging, chunk, ids_ref, lens_ref, sizes_ref, base_ref, *refs):
    q_refs, refs = refs[:units], refs[units:]
    k_ref, v_ref, refs = refs[0], refs[1], refs[2:]
    r_ref, refs = (refs[0], refs[1:]) if merging else (None, refs)
    o_ref, q_ref, p_ref, x_ref, a_ref, t_ref, h_ref, m_ref = refs
    unit = pl.program_id(0)
    request = ids_ref[unit]
    block = k_ref.shape[1]
    node_count = q_ref.shape[0]
    live = jnp.clip(lens_ref[request] - base_ref[0], 0, block)
    tiles = (sizes_ref[request] + NODES - 1) // NODES
    step = 256
    part = min(block, 512)
    part_chunks = (live + part - 1) // part

    def score(slot, at, width):
        return lax.dot_general(
            t_ref[slot],
            k_ref[0, pl.ds(at, width), :],
            (((1,), (1,)), ((), ())),
            preferred_element_type=jnp.float32,
        )

    def weigh(scores, slot):
        shift = h_ref[slot]
        return [
            jnp.exp2(scores[:, i : i + LANES] * exp2_scale - shift)
            for i in range(0, scores.shape[1], LANES)
        ]

    def masked(scores, at):
        column = lax.broadcasted_iota(jnp.int32, scores.shape, 1)
        return jnp.where(column < live - at, scores, negative_fill)

    def set_shift(slot, best):
        peaks = jnp.max(best, axis=1, keepdims=True) * exp2_scale
        h_ref[slot] = jnp.broadcast_to(peaks, best.shape)

    def take(t, slot):
        start = pl.multiple_of(t * NODES, NODES)
        for h in range(GROUP):
            t_ref[slot, h * NODES : (h + 1) * NODES, :] = q_ref[pl.ds(start, NODES), h * HD : (h + 1) * HD]

    def sample(t, slot):
        take(t, slot)
        set_shift(slot, masked(score(slot, 0, LANES), 0))

    def whole_block(slot):
        for c in range(0, block, chunk):
            for at in range(c, c + chunk, step):
                for i, piece in enumerate(weigh(score(slot, at, step), slot)):
                    p_ref[:, at + i * LANES : at + (i + 1) * LANES] = piece.astype(jnp.bfloat16)
            sums = jnp.dot(p_ref[:, c : c + chunk], x_ref[c : c + chunk, :], preferred_element_type=jnp.float32)
            a_ref[slot] = sums if c == 0 else a_ref[slot] + sums

    def part_block(slot):
        a_ref[slot] = jnp.zeros((ROWS, 2 * LANES), jnp.float32)

        @pl.loop(0, part_chunks)
        def _(c):
            at = pl.multiple_of(c * part, part)
            pieces = weigh(masked(score(slot, at, part), at), slot)
            weights = jnp.concatenate([piece.astype(jnp.bfloat16) for piece in pieces], axis=1)
            a_ref[slot] += jnp.dot(weights, x_ref[pl.ds(at, part), :], preferred_element_type=jnp.float32)

    def exact_shift(slot):
        a_ref[slot, :, :LANES] = jnp.full((ROWS, LANES), negative_fill, jnp.float32)

        @pl.loop(0, part_chunks)
        def _(c):
            at = pl.multiple_of(c * part, part)
            best = lane_max(masked(score(slot, at, part), at))
            a_ref[slot, :, :LANES] = jnp.maximum(a_ref[slot, :, :LANES], best)

        set_shift(slot, a_ref[slot, :, :LANES])

    def finish(t, slot):
        rows = pl.ds(pl.multiple_of(t * NODES, NODES), NODES)
        totals = a_ref[slot, :, LANES:]
        m_ref[...] = jnp.maximum(m_ref[...], totals)
        inverse = 1.0 / totals
        logs = h_ref[slot] * math.log(2.0) + jnp.log(totals)
        other_logs = join_logs(r_ref[0, rows, WIDE:]) if merging else None
        head_logs = []
        for h in range(GROUP):
            at = slice(h * NODES, (h + 1) * NODES)
            columns = slice(h * HD, (h + 1) * HD)
            partial = a_ref[slot, at, :LANES] * inverse[at]
            log = logs[at]
            if merging:
                other = jnp.broadcast_to(other_logs[:, h : h + 1], (NODES, LANES))
                top = jnp.maximum(log, other)
                own_weight = jnp.exp(log - top)
                other_weight = jnp.exp(other - top)
                total = own_weight + other_weight
                mixed = partial * own_weight + r_ref[0, rows, columns].astype(jnp.float32) * other_weight
                partial = mixed / total
                log = top + jnp.log(total)
            o_ref[0, rows, columns] = partial.astype(wire)
            head_logs.append(log)
        o_ref[0, rows, WIDE:] = split_logs(place_logs(head_logs))

    @pl.when(unit == 0)
    def _():
        x_ref[:, HD:] = jnp.ones((block, LANES), x_ref.dtype)
        a_ref[...] = jnp.ones(a_ref.shape, jnp.float32)
        h_ref[...] = jnp.zeros(h_ref.shape, jnp.float32)

    @pl.when(live == 0)
    def _():
        if merging:
            o_ref[...] = r_ref[...]
        else:
            o_ref[0, :, :WIDE] = jnp.zeros((node_count, WIDE), wire)
            o_ref[0, :, WIDE:] = split_logs(jnp.full((node_count, LANES), negative_fill, jnp.float32))

    @pl.when(live > 0)
    def _():
        for i in range(units):

            @pl.when(unit == i)
            def _():
                q_ref[...] = q_refs[i][...]

        x_ref[:, :HD] = v_ref[0]
        m_ref[...] = jnp.zeros(m_ref.shape, jnp.float32)

    @pl.when(jnp.logical_and(live > 0, live < block))
    def _():
        @pl.loop(0, tiles)
        def _(t):
            sample(t, 0)
            part_block(0)
            finish(t, 0)

    @pl.when(live == block)
    def _():
        sample(0, 0)

        @pl.loop(0, tiles)
        def _(t):
            slot = t % 2
            whole_block(slot)
            finish(jnp.maximum(t - 1, 0), 1 - slot)
            sample(jnp.minimum(t + 1, tiles - 1), 1 - slot)

        finish(tiles - 1, (tiles - 1) % 2)

    @pl.when(jnp.logical_and(live > 0, jnp.logical_not(jnp.max(m_ref[...]) < 2.0**100)))
    def _():
        @pl.loop(0, tiles)
        def _(t):
            take(t, 0)
            exact_shift(0)
            part_block(0)
            finish(t, 0)


def unit_attention(queries, ids, kv_heads, cache_keys, cache_values, lens, sizes, base, node_count, received=None):
    units = len(queries)
    block = cache_keys.shape[1]
    chunk = min(block, 1024)
    merging = received is not None
    scalars = jnp.concatenate([ids, jnp.asarray(kv_heads, jnp.int32)])
    width = WIDE + LANES

    def cache_map(u, ids_ref, *_):
        return (ids_ref[u], 0, ids_ref[units + u])

    def unit_map(u, *_):
        return (u, 0, 0)

    in_specs = [
        pl.BlockSpec((node_count, WIDE), functools.partial(lambda b, u, *_: (b, 0), rows)) for _, rows in queries
    ]
    in_specs += [pl.BlockSpec((1, block, HD), cache_map)] * 2
    operands = [array for array, _ in queries] + [cache_keys, cache_values]
    if merging:
        in_specs.append(pl.BlockSpec((1, node_count, width), unit_map))
        operands.append(received)
    grid_spec = pltpu.PrefetchScalarGridSpec(
        num_scalar_prefetch=4,
        grid=(units,),
        in_specs=in_specs,
        out_specs=pl.BlockSpec((1, node_count, width), unit_map),
        scratch_shapes=[
            pltpu.VMEM((node_count, WIDE), jnp.bfloat16),
            pltpu.VMEM((ROWS, block), jnp.bfloat16),
            pltpu.VMEM((block, 2 * LANES), jnp.bfloat16),
            pltpu.VMEM((2, ROWS, 2 * LANES), jnp.float32),
            pltpu.VMEM((2, ROWS, HD), jnp.bfloat16),
            pltpu.VMEM((2, ROWS, LANES), jnp.float32),
            pltpu.VMEM((ROWS, LANES), jnp.float32),
        ],
    )
    return pl.pallas_call(
        functools.partial(unit_kernel, units, merging, chunk),
        grid_spec=grid_spec,
        out_shape=jax.ShapeDtypeStruct((units, node_count, width), wire),
        compiler_params=pltpu.CompilerParams(vmem_limit_bytes=56 * 1024 * 1024),
        cost_estimate=pl.CostEstimate(
            flops=4 * units * node_count * GROUP * block * HD,
            bytes_accessed=units * (4 * block * HD + 4 * node_count * width),
            transcendentals=units * node_count * GROUP * block,
        ),
    )(scalars, lens, sizes, base, *operands)


def tree_kernel(first_ref, *refs):
    kv_local = len(refs) - 6
    q_refs = refs[:kv_local]
    k_ref, v_ref, parents_ref, o_ref, l_ref, r_ref = refs[kv_local:]
    rows_owned = q_refs[0].shape[0]
    node_count = k_ref.shape[0]
    steps = (node_count - 1).bit_length()
    node = lax.broadcasted_iota(jnp.int32, (node_count, node_count), 0)
    other = lax.broadcasted_iota(jnp.int32, (node_count, node_count), 1)
    linked = jnp.logical_or(parents_ref[...] == node, node == other)
    reached = linked.astype(jnp.float32)
    for _ in range(steps):
        half = reached.astype(jnp.bfloat16)
        reached = jnp.minimum(jnp.dot(half, half, preferred_element_type=jnp.float32), 1.0)
    r_ref[...] = reached.T
    tile = min(rows_owned, NODES)
    for g in range(kv_local):
        keys = k_ref[:, g * HD : (g + 1) * HD]
        values = v_ref[:, g * HD : (g + 1) * HD]

        @pl.loop(0, rows_owned // tile)
        def _(t):
            start = pl.multiple_of(t * tile, tile)
            first = pl.multiple_of(first_ref[0] + start, tile)
            queries = jnp.concatenate(
                [q_refs[g][pl.ds(start, tile), h * HD : (h + 1) * HD] for h in range(GROUP)], axis=0
            )
            live = jnp.concatenate([r_ref[pl.ds(first, tile), :]] * GROUP, axis=0) > 0.5
            scores = lax.dot_general(
                queries, keys, (((1,), (1,)), ((), ())), preferred_element_type=jnp.float32
            )
            scores = jnp.where(live, scores, negative_fill)
            peaks = jnp.max(scores, axis=1, keepdims=True)
            weights = jnp.where(live, jnp.exp2((scores - peaks) * exp2_scale), 0.0)
            totals = jnp.maximum(jnp.sum(weights, axis=1, keepdims=True), 1.0)
            sums = jnp.dot(weights.astype(jnp.bfloat16), values, preferred_element_type=jnp.float32)
            partials = sums / totals
            for h in range(GROUP):
                o_ref[g, pl.ds(start, tile), h * HD : (h + 1) * HD] = partials[h * tile : (h + 1) * tile, :]
            logs = jnp.broadcast_to(peaks * softmax_scale + jnp.log(totals), (GROUP * tile, LANES))
            l_ref[g, pl.ds(start, tile), :] = place_logs([logs[h * tile : (h + 1) * tile] for h in range(GROUP)])


def tree_attention(queries, keys, values, parents, first):
    rows = queries[0].shape[0]
    node_count = keys.shape[0]
    kv_local = len(queries)
    vmem = pl.BlockSpec(memory_space=pltpu.VMEM)
    return pl.pallas_call(
        tree_kernel,
        in_specs=[pl.BlockSpec(memory_space=pltpu.SMEM)] + [vmem] * (kv_local + 3),
        out_specs=[vmem, vmem],
        out_shape=[
            jax.ShapeDtypeStruct((kv_local, rows, WIDE), jnp.float32),
            jax.ShapeDtypeStruct((kv_local, rows, LANES), jnp.float32),
        ],
        scratch_shapes=[pltpu.VMEM((node_count, node_count), jnp.float32)],
        compiler_params=pltpu.CompilerParams(vmem_limit_bytes=32 * 1024 * 1024),
        cost_estimate=pl.CostEstimate(flops=10**9, bytes_accessed=10**7, transcendentals=10**6),
    )(first, *queries, keys, values, parents)


def merge_kernel(parts, alive_ref, *refs):
    kv_local = len(parts)
    o_ref = refs[-1]
    tree_ref, tree_logs_ref = refs[-3], refs[-2]
    at_part = 0
    for g in range(kv_local):
        part_refs = refs[at_part : at_part + parts[g]]
        at_part += parts[g]
        logs = [join_logs(ref[0, :, WIDE:]) for ref in part_refs] + [tree_logs_ref[g]]
        top = functools.reduce(jnp.maximum, logs)
        weights = [jnp.exp(log - top) for log in logs]
        scale = 1.0 / functools.reduce(jnp.add, weights)
        shares = [weight * scale for weight in weights]
        for h in range(GROUP):
            at = slice(h * HD, (h + 1) * HD)
            total = tree_ref[g, :, at] * shares[-1][:, h : h + 1]
            for ref, share in zip(part_refs, shares):
                total += ref[0, :, at].astype(jnp.float32) * share[:, h : h + 1]
            total = jnp.where(alive_ref[...] > 0.5, total, 0.0)
            o_ref[:, g * WIDE + h * HD : g * WIDE + (h + 1) * HD] = total.astype(o_ref.dtype)


def merge(parts, tree_partials, tree_logs, alive):
    kv_local, rows, _ = tree_partials.shape
    tile = min(rows, NODES)
    flat = [pair for of_head in parts for pair in of_head]
    return pl.pallas_call(
        functools.partial(merge_kernel, [len(of_head) for of_head in parts]),
        grid=(rows // tile,),
        in_specs=[pl.BlockSpec((tile, LANES), lambda i: (i, 0))]
        + [
            pl.BlockSpec((1, tile, WIDE + LANES), functools.partial(lambda u, i: (u, i, 0), unit))
            for _, unit in flat
        ]
        + [
            pl.BlockSpec((kv_local, tile, WIDE), lambda i: (0, i, 0)),
            pl.BlockSpec((kv_local, tile, LANES), lambda i: (0, i, 0)),
        ],
        out_specs=pl.BlockSpec((tile, kv_local * WIDE), lambda i: (i, 0)),
        out_shape=jax.ShapeDtypeStruct((rows, kv_local * WIDE), jnp.bfloat16),
        compiler_params=pltpu.CompilerParams(vmem_limit_bytes=48 * 1024 * 1024),
    )(alive, *[array for array, _ in flat], tree_partials, tree_logs)


def exchange(array, distance):
    owners = lax.axis_size("req")
    return lax.ppermute(array, "req", [(r, r ^ distance) for r in range(owners)])


def body(
    queries, cache_keys, cache_values, tree_keys, tree_values, parents, tree_sizes, cache_lens
):
    owner_index = lax.axis_index("req")
    owners = lax.axis_size("req")
    requests = cache_keys.shape[0]
    block = cache_keys.shape[1]
    kv_local = cache_keys.shape[2] // HD
    node_count = parents.shape[1]
    rows_owned = tree_keys.shape[0]
    head_devices = lax.axis_size("head")
    own = []
    for g in range(kv_local):
        columns = [
            queries[:, (d * kv_local + g) * WIDE : (d * kv_local + g + 1) * WIDE] for d in range(head_devices)
        ]
        mine = jnp.concatenate(columns, axis=1) if kv_local > 1 else queries
        own.append(lax.all_to_all(mine, "head", split_axis=1, concat_axis=0, tiled=True))

    first_row = owner_index * rows_owned
    request = first_row // node_count
    first_node = first_row % node_count
    if rows_owned < node_count:
        every_key = lax.all_gather(tree_keys, "req", axis=0, tiled=True)
        every_value = lax.all_gather(tree_values, "req", axis=0, tiled=True)
        own_keys = lax.dynamic_slice_in_dim(every_key, request * node_count, node_count, 0)
        own_values = lax.dynamic_slice_in_dim(every_value, request * node_count, node_count, 0)
    else:
        own_keys, own_values = tree_keys, tree_values
    own_parents = lax.dynamic_slice_in_dim(parents, request, 1, 0)

    def attend_tree(after=None):
        first = first_node[None]
        if after is not None:
            first, _ = lax.optimization_barrier((first, after))
        return tree_attention(own, own_keys, own_values, own_parents, first)

    size = lax.dynamic_index_in_dim(tree_sizes, request, 0, keepdims=False)
    alive = first_node + jnp.arange(rows_owned, dtype=jnp.int32) < size
    alive = jnp.broadcast_to(alive[:, None].astype(jnp.float32), (rows_owned, LANES))
    base = (owner_index * block)[None]

    def attend(queries, targets, kv_heads, received=None, after=None):
        ids = jnp.stack(targets).astype(jnp.int32)
        if after is not None:
            ids, _ = lax.optimization_barrier((ids, after))
        return unit_attention(
            queries, ids, kv_heads, cache_keys, cache_values, cache_lens, tree_sizes, base, node_count, received
        )

    if owners == 8 and rows_owned == node_count and kv_local == 2:
        sib = [exchange(q, 1) for q in own]
        x_own = [exchange(q, 2) for q in own]
        y_own = [exchange(q, 4) for q in own]
        x_sib = [exchange(q, 1) for q in x_own]
        y_sib = [exchange(q, 1) for q in y_own]
        d_own = [exchange(x_own[0], 4), exchange(y_own[1], 2)]
        d_sib = [exchange(q, 1) for q in d_own]
        r = owner_index
        out_a = attend([(own[0], 0), (sib[0], 0)], [r, r ^ 1], [0, 0])
        s0 = exchange(out_a[1:2], 1)
        tree_partials, tree_logs = attend_tree(out_a)
        out_b0 = attend([(x_sib[0], 0), (y_sib[0], 0)], [r ^ 3, r ^ 5], [0, 0], after=tree_logs)
        from_b0 = exchange(out_b0, 1)
        out_b1 = attend([(x_sib[1], 0), (y_sib[1], 0)], [r ^ 3, r ^ 5], [1, 1], after=out_b0)
        from_b1 = exchange(out_b1, 1)
        out_c0 = attend([(x_own[0], 0), (y_own[0], 0)], [r ^ 2, r ^ 4], [0, 0], from_b0, after=(out_b1, s0))
        x0, y0 = exchange(out_c0[0:1], 2), exchange(out_c0[1:2], 4)
        out_e = attend([(d_sib[0], 0), (d_sib[1], 0)], [r ^ 7, r ^ 7], [0, 1], after=out_c0)
        from_e = exchange(out_e, 1)
        out_c1 = attend([(x_own[1], 0), (y_own[1], 0)], [r ^ 2, r ^ 4], [1, 1], from_b1, after=out_e)
        x1, y1 = exchange(out_c1[0:1], 2), exchange(out_c1[1:2], 4)
        out_d = attend([(d_own[0], 0), (d_own[1], 0)], [r ^ 6, r ^ 6], [0, 1], from_e, after=(out_c1, x0, y0))
        diagonal = exchange(out_d, 6)
        out_f = attend([(own[1], 0), (sib[1], 0)], [r, r ^ 1], [1, 1], after=out_d)
        s1 = exchange(out_f[1:2], 1)
        parts = [
            [(out_a, 0), (s0, 0), (x0, 0), (y0, 0), (diagonal, 0)],
            [(out_f, 0), (s1, 0), (x1, 0), (y1, 0), (diagonal, 1)],
        ]
        return merge(parts, tree_partials, tree_logs, alive)

    tree_partials, tree_logs = attend_tree()
    every = [lax.all_gather(q, "req", axis=0, tiled=True) for q in own]
    units = [(g, a) for g in range(kv_local) for a in range(requests)]
    partials = attend(
        [(every[g], a) for g, a in units], [jnp.int32(a) for _, a in units], [g for g, _ in units]
    )
    partials = partials.reshape(kv_local, owners, rows_owned, WIDE + LANES)
    partials = lax.all_to_all(partials, "req", split_axis=1, concat_axis=1)
    partials = partials.reshape(kv_local * owners, rows_owned, WIDE + LANES)
    parts = [[(partials, g * owners + j) for j in range(owners)] for g in range(kv_local)]
    return merge(parts, tree_partials, tree_logs, alive)


def solution(mesh):
    placed = (
        P(("req", "head"), None),
        P(None, "req", "head"),
        P(None, "req", "head"),
        P("req", "head"),
        P("req", "head"),
        P(),
        P(),
        P(),
    )
    return jax.shard_map(
        body, mesh=mesh, in_specs=placed, out_specs=P("req", "head"), check_vma=False
    )
```

```python
import functools
import math

import jax
import jax.numpy as jnp
from jax import lax
from jax.experimental import pallas as pl
from jax.experimental.pallas import tpu as pltpu
from jax.sharding import PartitionSpec as P

NH = 128
KVH = 8
HD = 128
GROUP = NH // KVH
WIDE = GROUP * HD
LANES = 128
NODES = 32
ROWS = GROUP * NODES

negative_fill = -1e30
softmax_scale = 1.0 / math.sqrt(HD)
exp2_scale = softmax_scale * math.log2(math.e)
wire = jnp.bfloat16


def lane_max(scores):
    best = scores[:, :LANES]
    for at in range(LANES, scores.shape[1], LANES):
        best = jnp.maximum(best, scores[:, at : at + LANES])
    return best


def place_logs(logs):
    lane = lax.broadcasted_iota(jnp.int32, logs[0].shape, 1) % GROUP
    placed = logs[0]
    for head in range(1, GROUP):
        placed = jnp.where(lane == head, logs[head], placed)
    return placed


def split_logs(logs):
    high = logs.astype(wire).astype(jnp.float32)
    rest = logs - high
    middle = rest.astype(wire).astype(jnp.float32)
    group = lax.broadcasted_iota(jnp.int32, logs.shape, 1) // GROUP
    parts = jnp.where(group == 0, high, jnp.where(group == 1, middle, rest - middle))
    return parts.astype(wire)


def join_logs(parts):
    parts = parts.astype(jnp.float32)
    return parts + pltpu.roll(parts, LANES - GROUP, 1) + pltpu.roll(parts, LANES - 2 * GROUP, 1)


def unit_kernel(listed, merging, chunk, ids_ref, lens_ref, sizes_ref, base_ref, *refs):
    q_refs, refs = refs[:listed], refs[listed:]
    k_ref, v_ref, refs = refs[0], refs[1], refs[2:]
    r_ref, refs = (refs[0], refs[1:]) if merging else (None, refs)
    o_ref, q_ref, p_ref, x_ref, a_ref, t_ref, h_ref, m_ref = refs
    unit = pl.program_id(0)
    request = ids_ref[unit]
    block = k_ref.shape[1]
    node_count = q_ref.shape[0]
    live = jnp.clip(lens_ref[request] - base_ref[0], 0, block)
    tiles = (sizes_ref[request] + NODES - 1) // NODES
    step = 256
    part = min(block, 512)
    part_chunks = (live + part - 1) // part

    def score(slot, at, width):
        return lax.dot_general(
            t_ref[slot],
            k_ref[0, pl.ds(at, width), :],
            (((1,), (1,)), ((), ())),
            preferred_element_type=jnp.float32,
        )

    def weigh(scores, slot):
        shift = h_ref[slot]
        return [
            jnp.exp2(scores[:, i : i + LANES] * exp2_scale - shift)
            for i in range(0, scores.shape[1], LANES)
        ]

    def masked(scores, at):
        column = lax.broadcasted_iota(jnp.int32, scores.shape, 1)
        return jnp.where(column < live - at, scores, negative_fill)

    def set_shift(slot, best):
        peaks = jnp.max(best, axis=1, keepdims=True) * exp2_scale
        h_ref[slot] = jnp.broadcast_to(peaks, best.shape)

    def take(t, slot):
        start = pl.multiple_of(t * NODES, NODES)
        for h in range(GROUP):
            t_ref[slot, h * NODES : (h + 1) * NODES, :] = q_ref[pl.ds(start, NODES), h * HD : (h + 1) * HD]

    def sample(t, slot):
        take(t, slot)
        set_shift(slot, masked(score(slot, 0, LANES), 0))

    def whole_block(slot):
        for c in range(0, block, chunk):
            for at in range(c, c + chunk, step):
                for i, piece in enumerate(weigh(score(slot, at, step), slot)):
                    p_ref[:, at + i * LANES : at + (i + 1) * LANES] = piece.astype(jnp.bfloat16)
            sums = jnp.dot(p_ref[:, c : c + chunk], x_ref[c : c + chunk, :], preferred_element_type=jnp.float32)
            a_ref[slot] = sums if c == 0 else a_ref[slot] + sums

    def part_block(slot):
        a_ref[slot] = jnp.zeros((ROWS, 2 * LANES), jnp.float32)

        @pl.loop(0, part_chunks)
        def _(c):
            at = pl.multiple_of(c * part, part)
            pieces = weigh(masked(score(slot, at, part), at), slot)
            weights = jnp.concatenate([piece.astype(jnp.bfloat16) for piece in pieces], axis=1)
            a_ref[slot] += jnp.dot(weights, x_ref[pl.ds(at, part), :], preferred_element_type=jnp.float32)

    def exact_shift(slot):
        a_ref[slot, :, :LANES] = jnp.full((ROWS, LANES), negative_fill, jnp.float32)

        @pl.loop(0, part_chunks)
        def _(c):
            at = pl.multiple_of(c * part, part)
            best = lane_max(masked(score(slot, at, part), at))
            a_ref[slot, :, :LANES] = jnp.maximum(a_ref[slot, :, :LANES], best)

        set_shift(slot, a_ref[slot, :, :LANES])

    def finish(t, slot):
        rows = pl.ds(pl.multiple_of(jnp.maximum(t, 0) * NODES, NODES), NODES)
        totals = a_ref[slot, :, LANES:]
        m_ref[...] = jnp.maximum(m_ref[...], jnp.where(t >= 0, totals, 0.0))
        inverse = 1.0 / totals
        logs = h_ref[slot] * math.log(2.0) + jnp.log(totals)
        other_logs = join_logs(r_ref[0, rows, WIDE:]) if merging else None
        head_logs = []
        for h in range(GROUP):
            at = slice(h * NODES, (h + 1) * NODES)
            columns = slice(h * HD, (h + 1) * HD)
            partial = a_ref[slot, at, :LANES] * inverse[at]
            log = logs[at]
            if merging:
                other = jnp.broadcast_to(other_logs[:, h : h + 1], (NODES, LANES))
                top = jnp.maximum(log, other)
                own_weight = jnp.exp(log - top)
                other_weight = jnp.exp(other - top)
                total = own_weight + other_weight
                mixed = partial * own_weight + r_ref[0, rows, columns].astype(jnp.float32) * other_weight
                partial = mixed / total
                log = top + jnp.log(total)
            o_ref[0, rows, columns] = partial.astype(wire)
            head_logs.append(log)
        o_ref[0, rows, WIDE:] = split_logs(place_logs(head_logs))

    @pl.when(unit == 0)
    def _():
        x_ref[:, HD:] = jnp.ones((block, LANES), x_ref.dtype)

    @pl.when(live == 0)
    def _():
        if merging:
            o_ref[...] = r_ref[...]
        else:
            o_ref[0, :, :WIDE] = jnp.zeros((node_count, WIDE), wire)
            o_ref[0, :, WIDE:] = split_logs(jnp.full((node_count, LANES), negative_fill, jnp.float32))

    @pl.when(live > 0)
    def _():
        if listed == 1:
            q_ref[...] = q_refs[0][...]
        else:
            for i in range(listed):

                @pl.when(unit == i)
                def _():
                    q_ref[...] = q_refs[i][...]

        x_ref[:, :HD] = v_ref[0]
        m_ref[...] = jnp.zeros(m_ref.shape, jnp.float32)

    @pl.when(jnp.logical_and(live > 0, live < block))
    def _():
        @pl.loop(0, tiles)
        def _(t):
            sample(t, 0)
            part_block(0)
            finish(t, 0)

    @pl.when(live == block)
    def _():
        sample(0, 0)

        @pl.loop(0, tiles)
        def _(t):
            slot = t % 2
            whole_block(slot)
            finish(t - 1, 1 - slot)
            sample(jnp.minimum(t + 1, tiles - 1), 1 - slot)

        finish(tiles - 1, (tiles - 1) % 2)

    @pl.when(jnp.logical_and(live > 0, jnp.logical_not(jnp.max(m_ref[...]) < 2.0**100)))
    def _():
        @pl.loop(0, tiles)
        def _(t):
            take(t, 0)
            exact_shift(0)
            part_block(0)
            finish(t, 0)


def unit_attention(queries, ids, kv_head, cache_keys, cache_values, lens, sizes, base, node_count, received=None):
    units = ids.shape[0]
    block = cache_keys.shape[1]
    chunk = min(block, 1024)
    merging = received is not None
    width = WIDE + LANES

    def cache_map(u, ids_ref, *_):
        return (ids_ref[u], 0, kv_head)

    def unit_map(u, *_):
        return (u, 0, 0)

    if isinstance(queries, list):
        in_specs = [pl.BlockSpec((node_count, WIDE), lambda u, *_: (0, 0))] * units
    else:
        queries = [queries]
        in_specs = [pl.BlockSpec((node_count, WIDE), lambda u, ids_ref, *_: (ids_ref[u], 0))]
    operands = queries + [cache_keys, cache_values]
    in_specs = in_specs + [pl.BlockSpec((1, block, HD), cache_map)] * 2
    if merging:
        in_specs.append(pl.BlockSpec((1, node_count, width), unit_map))
        operands.append(received)
    grid_spec = pltpu.PrefetchScalarGridSpec(
        num_scalar_prefetch=4,
        grid=(units,),
        in_specs=in_specs,
        out_specs=pl.BlockSpec((1, node_count, width), unit_map),
        scratch_shapes=[
            pltpu.VMEM((node_count, WIDE), jnp.bfloat16),
            pltpu.VMEM((ROWS, block), jnp.bfloat16),
            pltpu.VMEM((block, 2 * LANES), jnp.bfloat16),
            pltpu.VMEM((2, ROWS, 2 * LANES), jnp.float32),
            pltpu.VMEM((2, ROWS, HD), jnp.bfloat16),
            pltpu.VMEM((2, ROWS, LANES), jnp.float32),
            pltpu.VMEM((ROWS, LANES), jnp.float32),
        ],
    )
    return pl.pallas_call(
        functools.partial(unit_kernel, len(queries), merging, chunk),
        grid_spec=grid_spec,
        out_shape=jax.ShapeDtypeStruct((units, node_count, width), wire),
        compiler_params=pltpu.CompilerParams(vmem_limit_bytes=48 * 1024 * 1024),
        cost_estimate=pl.CostEstimate(
            flops=4 * units * node_count * GROUP * block * HD,
            bytes_accessed=units * (4 * block * HD + 4 * node_count * width),
            transcendentals=units * node_count * GROUP * block,
        ),
    )(ids, lens, sizes, base, *operands)


def tree_kernel(first_ref, *refs):
    kv_local = len(refs) - 6
    q_refs = refs[:kv_local]
    k_ref, v_ref, parents_ref, o_ref, l_ref, r_ref = refs[kv_local:]
    rows_owned = q_refs[0].shape[0]
    node_count = k_ref.shape[0]
    steps = (node_count - 1).bit_length()
    node = lax.broadcasted_iota(jnp.int32, (node_count, node_count), 0)
    other = lax.broadcasted_iota(jnp.int32, (node_count, node_count), 1)
    linked = jnp.logical_or(parents_ref[...] == node, node == other)
    reached = linked.astype(jnp.float32)
    for _ in range(steps):
        half = reached.astype(jnp.bfloat16)
        reached = jnp.minimum(jnp.dot(half, half, preferred_element_type=jnp.float32), 1.0)
    r_ref[...] = reached.T
    tile = min(rows_owned, NODES)
    for g in range(kv_local):
        keys = k_ref[:, g * HD : (g + 1) * HD]
        values = v_ref[:, g * HD : (g + 1) * HD]

        @pl.loop(0, rows_owned // tile)
        def _(t):
            start = pl.multiple_of(t * tile, tile)
            first = pl.multiple_of(first_ref[0] + start, tile)
            queries = jnp.concatenate(
                [q_refs[g][pl.ds(start, tile), h * HD : (h + 1) * HD] for h in range(GROUP)], axis=0
            )
            live = jnp.concatenate([r_ref[pl.ds(first, tile), :]] * GROUP, axis=0) > 0.5
            scores = lax.dot_general(
                queries, keys, (((1,), (1,)), ((), ())), preferred_element_type=jnp.float32
            )
            scores = jnp.where(live, scores, negative_fill)
            peaks = jnp.max(scores, axis=1, keepdims=True)
            weights = jnp.where(live, jnp.exp2((scores - peaks) * exp2_scale), 0.0)
            totals = jnp.maximum(jnp.sum(weights, axis=1, keepdims=True), 1.0)
            sums = jnp.dot(weights.astype(jnp.bfloat16), values, preferred_element_type=jnp.float32)
            partials = sums / totals
            for h in range(GROUP):
                o_ref[g, pl.ds(start, tile), h * HD : (h + 1) * HD] = partials[h * tile : (h + 1) * tile, :]
            logs = jnp.broadcast_to(peaks * softmax_scale + jnp.log(totals), (GROUP * tile, LANES))
            l_ref[g, pl.ds(start, tile), :] = place_logs([logs[h * tile : (h + 1) * tile] for h in range(GROUP)])


def tree_attention(queries, keys, values, parents, first):
    rows = queries[0].shape[0]
    node_count = keys.shape[0]
    kv_local = len(queries)
    vmem = pl.BlockSpec(memory_space=pltpu.VMEM)
    return pl.pallas_call(
        tree_kernel,
        in_specs=[pl.BlockSpec(memory_space=pltpu.SMEM)] + [vmem] * (kv_local + 3),
        out_specs=[vmem, vmem],
        out_shape=[
            jax.ShapeDtypeStruct((kv_local, rows, WIDE), jnp.float32),
            jax.ShapeDtypeStruct((kv_local, rows, LANES), jnp.float32),
        ],
        scratch_shapes=[pltpu.VMEM((node_count, node_count), jnp.float32)],
        compiler_params=pltpu.CompilerParams(vmem_limit_bytes=32 * 1024 * 1024),
        cost_estimate=pl.CostEstimate(flops=10**9, bytes_accessed=10**7, transcendentals=10**6),
    )(first, *queries, keys, values, parents)


def merge_kernel(parts, alive_ref, *refs):
    kv_local = len(parts)
    o_ref = refs[-1]
    tree_ref, tree_logs_ref = refs[-3], refs[-2]
    rows = o_ref.shape[0]
    lane = lax.broadcasted_iota(jnp.int32, (LANES, WIDE), 0)
    head = lax.broadcasted_iota(jnp.int32, (LANES, WIDE), 1) // HD
    spread = jnp.logical_and(lane % GROUP == head, lane < 3 * GROUP).astype(jnp.bfloat16)
    group = lax.broadcasted_iota(jnp.int32, (rows, LANES), 1) // GROUP
    at_part = 0
    for g in range(kv_local):
        part_refs = refs[at_part : at_part + parts[g]]
        at_part += parts[g]
        logs = [join_logs(ref[0, :, WIDE:]) for ref in part_refs] + [tree_logs_ref[g]]
        top = functools.reduce(jnp.maximum, logs)
        weights = [jnp.exp(log - top) for log in logs]
        scale = 1.0 / functools.reduce(jnp.add, weights)
        total = None
        for j, weight in enumerate(weights):
            share = jnp.where(group == 0, weight * scale, 0.0)
            share = share + pltpu.roll(share, GROUP, 1) + pltpu.roll(share, 2 * GROUP, 1)
            wide = jnp.dot(split_logs(share), spread, preferred_element_type=jnp.float32)
            piece = tree_ref[g] if j == parts[g] else part_refs[j][0, :, :WIDE].astype(jnp.float32)
            total = wide * piece if total is None else total + wide * piece
        alive = alive_ref[:, :1] > 0.5
        o_ref[:, g * WIDE : (g + 1) * WIDE] = jnp.where(alive, total, 0.0).astype(o_ref.dtype)


def merge(parts, tree_partials, tree_logs, alive):
    kv_local, rows, _ = tree_partials.shape
    tile = min(rows, NODES)
    flat = [pair for of_head in parts for pair in of_head]
    return pl.pallas_call(
        functools.partial(merge_kernel, [len(of_head) for of_head in parts]),
        grid=(rows // tile,),
        in_specs=[pl.BlockSpec((tile, LANES), lambda i: (i, 0))]
        + [
            pl.BlockSpec((1, tile, WIDE + LANES), functools.partial(lambda u, i: (u, i, 0), unit))
            for _, unit in flat
        ]
        + [
            pl.BlockSpec((kv_local, tile, WIDE), lambda i: (0, i, 0)),
            pl.BlockSpec((kv_local, tile, LANES), lambda i: (0, i, 0)),
        ],
        out_specs=pl.BlockSpec((tile, kv_local * WIDE), lambda i: (i, 0)),
        out_shape=jax.ShapeDtypeStruct((rows, kv_local * WIDE), jnp.bfloat16),
        compiler_params=pltpu.CompilerParams(vmem_limit_bytes=48 * 1024 * 1024),
    )(alive, *[array for array, _ in flat], tree_partials, tree_logs)


def exchange(array, distance):
    owners = lax.axis_size("req")
    return lax.ppermute(array, "req", [(r, r ^ distance) for r in range(owners)])


def body(
    queries, cache_keys, cache_values, tree_keys, tree_values, parents, tree_sizes, cache_lens
):
    owner_index = lax.axis_index("req")
    owners = lax.axis_size("req")
    requests = cache_keys.shape[0]
    block = cache_keys.shape[1]
    kv_local = cache_keys.shape[2] // HD
    node_count = parents.shape[1]
    rows_owned = tree_keys.shape[0]
    head_devices = lax.axis_size("head")
    own = []
    for g in range(kv_local):
        columns = [
            queries[:, (d * kv_local + g) * WIDE : (d * kv_local + g + 1) * WIDE] for d in range(head_devices)
        ]
        mine = jnp.concatenate(columns, axis=1) if kv_local > 1 else queries
        own.append(lax.all_to_all(mine, "head", split_axis=1, concat_axis=0, tiled=True))

    first_row = owner_index * rows_owned
    request = first_row // node_count
    first_node = first_row % node_count
    if rows_owned < node_count:
        every_key = lax.all_gather(tree_keys, "req", axis=0, tiled=True)
        every_value = lax.all_gather(tree_values, "req", axis=0, tiled=True)
        own_keys = lax.dynamic_slice_in_dim(every_key, request * node_count, node_count, 0)
        own_values = lax.dynamic_slice_in_dim(every_value, request * node_count, node_count, 0)
    else:
        own_keys, own_values = tree_keys, tree_values
    own_parents = lax.dynamic_slice_in_dim(parents, request, 1, 0)

    def attend_tree(after=None):
        first = first_node[None]
        if after is not None:
            first, _ = lax.optimization_barrier((first, after))
        return tree_attention(own, own_keys, own_values, own_parents, first)

    size = lax.dynamic_index_in_dim(tree_sizes, request, 0, keepdims=False)
    alive = first_node + jnp.arange(rows_owned, dtype=jnp.int32) < size
    alive = jnp.broadcast_to(alive[:, None].astype(jnp.float32), (rows_owned, LANES))
    base = (owner_index * block)[None]

    def attend(queries, targets, kv_head, received=None, after=None):
        ids = jnp.stack(targets).astype(jnp.int32)
        if after is not None:
            ids, _ = lax.optimization_barrier((ids, after))
        return unit_attention(
            queries, ids, kv_head, cache_keys, cache_values, cache_lens, tree_sizes, base, node_count, received
        )

    if owners == 8 and rows_owned == node_count and kv_local == 2:
        r = owner_index
        theirs, ours = [r ^ 3, r ^ 5, r ^ 7], [r ^ 2, r ^ 4, r ^ 6]

        def send(partials):
            return [exchange(partials[i : i + 1], 2 * (i + 1)) for i in range(3)]

        first = lax.all_gather(own[0], "req", axis=0, tiled=True)
        near0 = attend([own[0], exchange(own[0], 1)], [r, r ^ 1], 0)
        late, _ = lax.optimization_barrier((own[1], near0))
        second = lax.all_gather(late, "req", axis=0, tiled=True)
        from_near0 = exchange(near0[1:2], 1)
        tree_partials, tree_logs = attend_tree(near0)
        theirs0 = attend(first, theirs, 0, after=(tree_logs, from_near0))
        swapped0 = exchange(theirs0, 1)
        theirs1 = attend(second, theirs, 1, after=theirs0)
        swapped1 = exchange(theirs1, 1)
        ours0 = attend(first, ours, 0, swapped0, after=theirs1)
        sent0 = send(ours0)
        ours1 = attend(second, ours, 1, swapped1, after=ours0)
        sent1 = send(ours1)
        near1 = attend(second, [r, r ^ 1], 1, after=(ours1, sent0))
        from_near1 = exchange(near1[1:2], 1)
        parts = [
            [(near0, 0), (from_near0, 0)] + [(piece, 0) for piece in sent0],
            [(near1, 0), (from_near1, 0)] + [(piece, 0) for piece in sent1],
        ]
        return merge(parts, tree_partials, tree_logs, alive)

    tree_partials, tree_logs = attend_tree()
    every = [lax.all_gather(q, "req", axis=0, tiled=True) for q in own]
    targets = [jnp.int32(a) for a in range(requests)]
    partials = jnp.stack([attend(every[g], targets, g) for g in range(kv_local)])
    partials = partials.reshape(kv_local, owners, rows_owned, WIDE + LANES)
    partials = lax.all_to_all(partials, "req", split_axis=1, concat_axis=1)
    partials = partials.reshape(kv_local * owners, rows_owned, WIDE + LANES)
    parts = [[(partials, g * owners + j) for j in range(owners)] for g in range(kv_local)]
    return merge(parts, tree_partials, tree_logs, alive)


def solution(mesh):
    placed = (
        P(("req", "head"), None),
        P(None, "req", "head"),
        P(None, "req", "head"),
        P("req", "head"),
        P("req", "head"),
        P(),
        P(),
        P(),
    )
    return jax.shard_map(
        body, mesh=mesh, in_specs=placed, out_specs=P("req", "head"), check_vma=False
    )
```

```python
import functools
import math

import jax
import jax.numpy as jnp
from jax import lax
from jax.experimental import pallas as pl
from jax.experimental.pallas import tpu as pltpu
from jax.sharding import PartitionSpec as P

NH = 128
KVH = 8
HD = 128
GROUP = NH // KVH
WIDE = GROUP * HD
LANES = 128
NODES = 32
ROWS = GROUP * NODES

negative_fill = -1e30
softmax_scale = 1.0 / math.sqrt(HD)
exp2_scale = softmax_scale * math.log2(math.e)
wire = jnp.bfloat16


def lane_max(scores):
    best = scores[:, :LANES]
    for at in range(LANES, scores.shape[1], LANES):
        best = jnp.maximum(best, scores[:, at : at + LANES])
    return best


def place_logs(logs):
    lane = lax.broadcasted_iota(jnp.int32, logs[0].shape, 1) % GROUP
    placed = logs[0]
    for head in range(1, GROUP):
        placed = jnp.where(lane == head, logs[head], placed)
    return placed


def split_logs(logs):
    high = logs.astype(wire).astype(jnp.float32)
    rest = logs - high
    middle = rest.astype(wire).astype(jnp.float32)
    group = lax.broadcasted_iota(jnp.int32, logs.shape, 1) // GROUP
    parts = jnp.where(group == 0, high, jnp.where(group == 1, middle, rest - middle))
    return parts.astype(wire)


def join_logs(parts):
    parts = parts.astype(jnp.float32)
    return parts + pltpu.roll(parts, LANES - GROUP, 1) + pltpu.roll(parts, LANES - 2 * GROUP, 1)


def unit_kernel(listed, merging, chunk, ids_ref, lens_ref, sizes_ref, base_ref, *refs):
    q_refs, refs = refs[:listed], refs[listed:]
    k_ref, v_ref, refs = refs[0], refs[1], refs[2:]
    r_ref, refs = (refs[0], refs[1:]) if merging else (None, refs)
    o_ref, q_ref, p_ref, x_ref, a_ref, t_ref, h_ref, m_ref = refs
    unit = pl.program_id(0)
    request = ids_ref[unit]
    block = k_ref.shape[1]
    node_count = q_ref.shape[0]
    live = jnp.clip(lens_ref[request] - base_ref[0], 0, block)
    tiles = (sizes_ref[request] + NODES - 1) // NODES
    step = 256
    part = min(block, 512)
    part_chunks = (live + part - 1) // part

    def score(slot, at, width):
        return lax.dot_general(
            t_ref[slot],
            k_ref[0, pl.ds(at, width), :],
            (((1,), (1,)), ((), ())),
            preferred_element_type=jnp.float32,
        )

    def weigh(scores, slot):
        shift = h_ref[slot]
        return [
            jnp.exp2(scores[:, i : i + LANES] * exp2_scale - shift)
            for i in range(0, scores.shape[1], LANES)
        ]

    def masked(scores, at):
        column = lax.broadcasted_iota(jnp.int32, scores.shape, 1)
        return jnp.where(column < live - at, scores, negative_fill)

    def set_shift(slot, best):
        peaks = jnp.max(best, axis=1, keepdims=True) * exp2_scale
        h_ref[slot] = jnp.broadcast_to(peaks, best.shape)

    def take(t, slot):
        start = pl.multiple_of(t * NODES, NODES)
        for h in range(GROUP):
            t_ref[slot, h * NODES : (h + 1) * NODES, :] = q_ref[pl.ds(start, NODES), h * HD : (h + 1) * HD]

    def sample(t, slot):
        take(t, slot)
        set_shift(slot, masked(score(slot, 0, LANES), 0))

    def whole_block(slot):
        for c in range(0, block, chunk):
            for at in range(c, c + chunk, step):
                for i, piece in enumerate(weigh(score(slot, at, step), slot)):
                    p_ref[:, at + i * LANES : at + (i + 1) * LANES] = piece.astype(jnp.bfloat16)
            sums = jnp.dot(p_ref[:, c : c + chunk], x_ref[c : c + chunk, :], preferred_element_type=jnp.float32)
            a_ref[slot] = sums if c == 0 else a_ref[slot] + sums

    def part_block(slot):
        a_ref[slot] = jnp.zeros((ROWS, 2 * LANES), jnp.float32)

        @pl.loop(0, part_chunks)
        def _(c):
            at = pl.multiple_of(c * part, part)
            pieces = weigh(masked(score(slot, at, part), at), slot)
            weights = jnp.concatenate([piece.astype(jnp.bfloat16) for piece in pieces], axis=1)
            a_ref[slot] += jnp.dot(weights, x_ref[pl.ds(at, part), :], preferred_element_type=jnp.float32)

    def exact_shift(slot):
        a_ref[slot, :, :LANES] = jnp.full((ROWS, LANES), negative_fill, jnp.float32)

        @pl.loop(0, part_chunks)
        def _(c):
            at = pl.multiple_of(c * part, part)
            best = lane_max(masked(score(slot, at, part), at))
            a_ref[slot, :, :LANES] = jnp.maximum(a_ref[slot, :, :LANES], best)

        set_shift(slot, a_ref[slot, :, :LANES])

    def finish(t, slot):
        rows = pl.ds(pl.multiple_of(jnp.maximum(t, 0) * NODES, NODES), NODES)
        totals = a_ref[slot, :, LANES:]
        m_ref[...] = jnp.maximum(m_ref[...], jnp.where(t >= 0, totals, 0.0))
        inverse = 1.0 / totals
        logs = h_ref[slot] * math.log(2.0) + jnp.log(totals)
        other_logs = join_logs(r_ref[0, rows, WIDE:]) if merging else None
        head_logs = []
        for h in range(GROUP):
            at = slice(h * NODES, (h + 1) * NODES)
            columns = slice(h * HD, (h + 1) * HD)
            partial = a_ref[slot, at, :LANES] * inverse[at]
            log = logs[at]
            if merging:
                other = jnp.broadcast_to(other_logs[:, h : h + 1], (NODES, LANES))
                top = jnp.maximum(log, other)
                own_weight = jnp.exp(log - top)
                other_weight = jnp.exp(other - top)
                total = own_weight + other_weight
                mixed = partial * own_weight + r_ref[0, rows, columns].astype(jnp.float32) * other_weight
                partial = mixed / total
                log = top + jnp.log(total)
            o_ref[0, rows, columns] = partial.astype(wire)
            head_logs.append(log)
        o_ref[0, rows, WIDE:] = split_logs(place_logs(head_logs))

    @pl.when(unit == 0)
    def _():
        x_ref[:, HD:] = jnp.ones((block, LANES), x_ref.dtype)

    @pl.when(live == 0)
    def _():
        if merging:
            o_ref[...] = r_ref[...]
        else:
            o_ref[0, :, :WIDE] = jnp.zeros((node_count, WIDE), wire)
            o_ref[0, :, WIDE:] = split_logs(jnp.full((node_count, LANES), negative_fill, jnp.float32))

    @pl.when(live > 0)
    def _():
        if listed == 1:
            q_ref[...] = q_refs[0][...]
        else:
            for i in range(listed):

                @pl.when(unit == i)
                def _():
                    q_ref[...] = q_refs[i][...]

        x_ref[:, :HD] = v_ref[0]
        m_ref[...] = jnp.zeros(m_ref.shape, jnp.float32)

    @pl.when(jnp.logical_and(live > 0, live < block))
    def _():
        @pl.loop(0, tiles)
        def _(t):
            sample(t, 0)
            part_block(0)
            finish(t, 0)

    @pl.when(live == block)
    def _():
        sample(0, 0)

        @pl.loop(0, tiles)
        def _(t):
            slot = t % 2
            whole_block(slot)
            finish(t - 1, 1 - slot)
            sample(jnp.minimum(t + 1, tiles - 1), 1 - slot)

        finish(tiles - 1, (tiles - 1) % 2)

    @pl.when(jnp.logical_and(live > 0, jnp.logical_not(jnp.max(m_ref[...]) < 2.0**100)))
    def _():
        @pl.loop(0, tiles)
        def _(t):
            take(t, 0)
            exact_shift(0)
            part_block(0)
            finish(t, 0)


def unit_attention(queries, ids, kv_head, cache_keys, cache_values, lens, sizes, base, node_count, received=None):
    units = ids.shape[0] // 2
    block = cache_keys.shape[1]
    chunk = min(block, 1024)
    merging = received is not None
    width = WIDE + LANES

    def cache_map(u, ids_ref, *_):
        return (ids_ref[u], 0, kv_head)

    def unit_map(u, *_):
        return (u, 0, 0)

    def received_map(u, ids_ref, *_):
        return (ids_ref[2 * units] + u, 0, 0)

    if isinstance(queries, list):
        in_specs = [pl.BlockSpec((node_count, WIDE), lambda u, *_: (0, 0))] * units
    else:
        queries = [queries]
        in_specs = [pl.BlockSpec((node_count, WIDE), lambda u, ids_ref, *_: (ids_ref[units + u], 0))]
    operands = queries + [cache_keys, cache_values]
    in_specs = in_specs + [pl.BlockSpec((1, block, HD), cache_map)] * 2
    if merging:
        in_specs.append(pl.BlockSpec((1, node_count, width), received_map))
        operands.append(received)
    grid_spec = pltpu.PrefetchScalarGridSpec(
        num_scalar_prefetch=4,
        grid=(units,),
        in_specs=in_specs,
        out_specs=pl.BlockSpec((1, node_count, width), unit_map),
        scratch_shapes=[
            pltpu.VMEM((node_count, WIDE), jnp.bfloat16),
            pltpu.VMEM((ROWS, block), jnp.bfloat16),
            pltpu.VMEM((block, 2 * LANES), jnp.bfloat16),
            pltpu.VMEM((2, ROWS, 2 * LANES), jnp.float32),
            pltpu.VMEM((2, ROWS, HD), jnp.bfloat16),
            pltpu.VMEM((2, ROWS, LANES), jnp.float32),
            pltpu.VMEM((ROWS, LANES), jnp.float32),
        ],
    )
    return pl.pallas_call(
        functools.partial(unit_kernel, len(queries), merging, chunk),
        grid_spec=grid_spec,
        out_shape=jax.ShapeDtypeStruct((units, node_count, width), wire),
        compiler_params=pltpu.CompilerParams(vmem_limit_bytes=48 * 1024 * 1024),
        cost_estimate=pl.CostEstimate(
            flops=4 * units * node_count * GROUP * block * HD,
            bytes_accessed=units * (4 * block * HD + 4 * node_count * width),
            transcendentals=units * node_count * GROUP * block,
        ),
    )(ids, lens, sizes, base, *operands)


def tree_kernel(first_ref, *refs):
    kv_local = len(refs) - 6
    q_refs = refs[:kv_local]
    k_ref, v_ref, parents_ref, o_ref, l_ref, r_ref = refs[kv_local:]
    rows_owned = q_refs[0].shape[0]
    node_count = k_ref.shape[0]
    steps = (node_count - 1).bit_length()
    node = lax.broadcasted_iota(jnp.int32, (node_count, node_count), 0)
    other = lax.broadcasted_iota(jnp.int32, (node_count, node_count), 1)
    linked = jnp.logical_or(parents_ref[...] == node, node == other)
    reached = linked.astype(jnp.float32)
    for _ in range(steps):
        half = reached.astype(jnp.bfloat16)
        reached = jnp.minimum(jnp.dot(half, half, preferred_element_type=jnp.float32), 1.0)
    r_ref[...] = reached.T
    tile = min(rows_owned, NODES)
    for g in range(kv_local):
        keys = k_ref[:, g * HD : (g + 1) * HD]
        values = v_ref[:, g * HD : (g + 1) * HD]

        @pl.loop(0, rows_owned // tile)
        def _(t):
            start = pl.multiple_of(t * tile, tile)
            first = pl.multiple_of(first_ref[0] + start, tile)
            queries = jnp.concatenate(
                [q_refs[g][pl.ds(start, tile), h * HD : (h + 1) * HD] for h in range(GROUP)], axis=0
            )
            live = jnp.concatenate([r_ref[pl.ds(first, tile), :]] * GROUP, axis=0) > 0.5
            scores = lax.dot_general(
                queries, keys, (((1,), (1,)), ((), ())), preferred_element_type=jnp.float32
            )
            scores = jnp.where(live, scores, negative_fill)
            peaks = jnp.max(scores, axis=1, keepdims=True)
            weights = jnp.where(live, jnp.exp2((scores - peaks) * exp2_scale), 0.0)
            totals = jnp.maximum(jnp.sum(weights, axis=1, keepdims=True), 1.0)
            sums = jnp.dot(weights.astype(jnp.bfloat16), values, preferred_element_type=jnp.float32)
            partials = sums / totals
            for h in range(GROUP):
                o_ref[g, pl.ds(start, tile), h * HD : (h + 1) * HD] = partials[h * tile : (h + 1) * tile, :]
            logs = jnp.broadcast_to(peaks * softmax_scale + jnp.log(totals), (GROUP * tile, LANES))
            l_ref[g, pl.ds(start, tile), :] = place_logs([logs[h * tile : (h + 1) * tile] for h in range(GROUP)])


def tree_attention(queries, keys, values, parents, first):
    rows = queries[0].shape[0]
    node_count = keys.shape[0]
    kv_local = len(queries)
    vmem = pl.BlockSpec(memory_space=pltpu.VMEM)
    return pl.pallas_call(
        tree_kernel,
        in_specs=[pl.BlockSpec(memory_space=pltpu.SMEM)] + [vmem] * (kv_local + 3),
        out_specs=[vmem, vmem],
        out_shape=[
            jax.ShapeDtypeStruct((kv_local, rows, WIDE), jnp.float32),
            jax.ShapeDtypeStruct((kv_local, rows, LANES), jnp.float32),
        ],
        scratch_shapes=[pltpu.VMEM((node_count, node_count), jnp.float32)],
        compiler_params=pltpu.CompilerParams(vmem_limit_bytes=32 * 1024 * 1024),
        cost_estimate=pl.CostEstimate(flops=10**9, bytes_accessed=10**7, transcendentals=10**6),
    )(first, *queries, keys, values, parents)


def merge_kernel(parts, alive_ref, *refs):
    kv_local = len(parts)
    o_ref = refs[-1]
    tree_ref, tree_logs_ref = refs[-3], refs[-2]
    rows = o_ref.shape[0]
    lane = lax.broadcasted_iota(jnp.int32, (LANES, WIDE), 0)
    head = lax.broadcasted_iota(jnp.int32, (LANES, WIDE), 1) // HD
    spread = jnp.logical_and(lane % GROUP == head, lane < 3 * GROUP).astype(jnp.bfloat16)
    group = lax.broadcasted_iota(jnp.int32, (rows, LANES), 1) // GROUP
    at_part = 0
    for g in range(kv_local):
        part_refs = refs[at_part : at_part + parts[g]]
        at_part += parts[g]
        logs = [join_logs(ref[0, :, WIDE:]) for ref in part_refs] + [tree_logs_ref[g]]
        top = functools.reduce(jnp.maximum, logs)
        weights = [jnp.exp(log - top) for log in logs]
        scale = 1.0 / functools.reduce(jnp.add, weights)
        total = None
        for j, weight in enumerate(weights):
            share = jnp.where(group == 0, weight * scale, 0.0)
            share = share + pltpu.roll(share, GROUP, 1) + pltpu.roll(share, 2 * GROUP, 1)
            wide = jnp.dot(split_logs(share), spread, preferred_element_type=jnp.float32)
            piece = tree_ref[g] if j == parts[g] else part_refs[j][0, :, :WIDE].astype(jnp.float32)
            total = wide * piece if total is None else total + wide * piece
        alive = alive_ref[:, :1] > 0.5
        o_ref[:, g * WIDE : (g + 1) * WIDE] = jnp.where(alive, total, 0.0).astype(o_ref.dtype)


def merge(parts, tree_partials, tree_logs, alive):
    kv_local, rows, _ = tree_partials.shape
    tile = min(rows, NODES)
    flat = [pair for of_head in parts for pair in of_head]
    return pl.pallas_call(
        functools.partial(merge_kernel, [len(of_head) for of_head in parts]),
        grid=(rows // tile,),
        in_specs=[pl.BlockSpec((tile, LANES), lambda i: (i, 0))]
        + [
            pl.BlockSpec((1, tile, WIDE + LANES), functools.partial(lambda u, i: (u, i, 0), unit))
            for _, unit in flat
        ]
        + [
            pl.BlockSpec((kv_local, tile, WIDE), lambda i: (0, i, 0)),
            pl.BlockSpec((kv_local, tile, LANES), lambda i: (0, i, 0)),
        ],
        out_specs=pl.BlockSpec((tile, kv_local * WIDE), lambda i: (i, 0)),
        out_shape=jax.ShapeDtypeStruct((rows, kv_local * WIDE), jnp.bfloat16),
        compiler_params=pltpu.CompilerParams(vmem_limit_bytes=48 * 1024 * 1024),
    )(alive, *[array for array, _ in flat], tree_partials, tree_logs)


def exchange(array, distance):
    owners = lax.axis_size("req")
    return lax.ppermute(array, "req", [(r, r ^ distance) for r in range(owners)])


def body(
    queries, cache_keys, cache_values, tree_keys, tree_values, parents, tree_sizes, cache_lens
):
    owner_index = lax.axis_index("req")
    owners = lax.axis_size("req")
    requests = cache_keys.shape[0]
    block = cache_keys.shape[1]
    kv_local = cache_keys.shape[2] // HD
    node_count = parents.shape[1]
    rows_owned = tree_keys.shape[0]
    head_devices = lax.axis_size("head")
    own = []
    for g in range(kv_local):
        columns = [
            queries[:, (d * kv_local + g) * WIDE : (d * kv_local + g + 1) * WIDE] for d in range(head_devices)
        ]
        mine = jnp.concatenate(columns, axis=1) if kv_local > 1 else queries
        own.append(lax.all_to_all(mine, "head", split_axis=1, concat_axis=0, tiled=True))

    first_row = owner_index * rows_owned
    request = first_row // node_count
    first_node = first_row % node_count
    if rows_owned < node_count:
        every_key = lax.all_gather(tree_keys, "req", axis=0, tiled=True)
        every_value = lax.all_gather(tree_values, "req", axis=0, tiled=True)
        own_keys = lax.dynamic_slice_in_dim(every_key, request * node_count, node_count, 0)
        own_values = lax.dynamic_slice_in_dim(every_value, request * node_count, node_count, 0)
    else:
        own_keys, own_values = tree_keys, tree_values
    own_parents = lax.dynamic_slice_in_dim(parents, request, 1, 0)

    def attend_tree(after=None):
        first = first_node[None]
        if after is not None:
            first, _ = lax.optimization_barrier((first, after))
        return tree_attention(own, own_keys, own_values, own_parents, first)

    size = lax.dynamic_index_in_dim(tree_sizes, request, 0, keepdims=False)
    alive = first_node + jnp.arange(rows_owned, dtype=jnp.int32) < size
    alive = jnp.broadcast_to(alive[:, None].astype(jnp.float32), (rows_owned, LANES))
    base = (owner_index * block)[None]

    def attend(queries, targets, blocks, kv_head, received=None, offset=0, after=None):
        ids = jnp.stack([jnp.asarray(i, jnp.int32) for i in [*targets, *blocks, offset]])
        if after is not None:
            ids, _ = lax.optimization_barrier((ids, after))
        return unit_attention(
            queries, ids, kv_head, cache_keys, cache_values, cache_lens, tree_sizes, base, node_count, received
        )

    if owners == 8 and rows_owned == node_count and kv_local == 2:
        r = owner_index
        chip, core = r // 2, r % 2
        cores = [[2 * i, 2 * i + 1] for i in range(4)]
        chips = [[0, 2, 4, 6], [1, 3, 5, 7]]
        ours, theirs = [r ^ 2, r ^ 4, r ^ 6], [r ^ 3, r ^ 5, r ^ 7]
        our_blocks = [chip ^ 1, chip ^ 2, chip ^ 3]
        their_blocks = [4 * (1 - core) + block for block in our_blocks]

        def gather(array, groups):
            return lax.all_gather(array, "req", axis=0, tiled=True, axis_index_groups=groups)

        def send(partials):
            return [exchange(partials[i : i + 1], 2 * (i + 1) + 1) for i in range(3)]

        first = gather(own[0], chips)
        near0 = attend([own[0], exchange(own[0], 1)], [r, r ^ 1], [0, 0], 0)
        first_all = gather(first, cores)
        late, _ = lax.optimization_barrier((own[1], near0))
        second = gather(late, chips)
        second_all = gather(second, cores)
        from_near0 = exchange(near0[1:2], 1)
        tree_partials, tree_logs = attend_tree(near0)
        ours0 = attend(first, ours, our_blocks, 0, after=(tree_logs, from_near0))
        swapped0 = gather(ours0, cores)
        ours1 = attend(second, ours, our_blocks, 1, after=ours0)
        swapped1 = gather(ours1, cores)
        sibling_part = 3 * (1 - core)
        theirs0 = attend(first_all, theirs, their_blocks, 0, swapped0, sibling_part, after=ours1)
        sent0 = send(theirs0)
        theirs1 = attend(second_all, theirs, their_blocks, 1, swapped1, sibling_part, after=theirs0)
        sent1 = send(theirs1)
        near1 = attend(second_all, [r, r ^ 1], [4 * core + chip, 4 * (1 - core) + chip], 1, after=(theirs1, sent0))
        from_near1 = exchange(near1[1:2], 1)
        parts = [
            [(near0, 0), (from_near0, 0)] + [(piece, 0) for piece in sent0],
            [(near1, 0), (from_near1, 0)] + [(piece, 0) for piece in sent1],
        ]
        return merge(parts, tree_partials, tree_logs, alive)

    tree_partials, tree_logs = attend_tree()
    every = [lax.all_gather(q, "req", axis=0, tiled=True) for q in own]
    targets = list(range(requests))
    partials = jnp.stack([attend(every[g], targets, targets, g) for g in range(kv_local)])
    partials = partials.reshape(kv_local, owners, rows_owned, WIDE + LANES)
    partials = lax.all_to_all(partials, "req", split_axis=1, concat_axis=1)
    partials = partials.reshape(kv_local * owners, rows_owned, WIDE + LANES)
    parts = [[(partials, g * owners + j) for j in range(owners)] for g in range(kv_local)]
    return merge(parts, tree_partials, tree_logs, alive)


def solution(mesh):
    placed = (
        P(("req", "head"), None),
        P(None, "req", "head"),
        P(None, "req", "head"),
        P("req", "head"),
        P("req", "head"),
        P(),
        P(),
        P(),
    )
    return jax.shard_map(
        body, mesh=mesh, in_specs=placed, out_specs=P("req", "head"), check_vma=False
    )
```

```python
import functools
import math

import jax
import jax.numpy as jnp
from jax import lax
from jax.experimental import pallas as pl
from jax.experimental.pallas import tpu as pltpu
from jax.sharding import PartitionSpec as P

NH = 128
KVH = 8
HD = 128
GROUP = NH // KVH
WIDE = GROUP * HD
LANES = 128
NODES = 32
ROWS = GROUP * NODES

negative_fill = -1e30
softmax_scale = 1.0 / math.sqrt(HD)
exp2_scale = softmax_scale * math.log2(math.e)
wire = jnp.bfloat16


def lane_max(scores):
    best = scores[:, :LANES]
    for at in range(LANES, scores.shape[1], LANES):
        best = jnp.maximum(best, scores[:, at : at + LANES])
    return best


def place_logs(logs):
    lane = lax.broadcasted_iota(jnp.int32, logs[0].shape, 1) % GROUP
    placed = logs[0]
    for head in range(1, GROUP):
        placed = jnp.where(lane == head, logs[head], placed)
    return placed


def split_logs(logs):
    high = logs.astype(wire).astype(jnp.float32)
    rest = logs - high
    middle = rest.astype(wire).astype(jnp.float32)
    group = lax.broadcasted_iota(jnp.int32, logs.shape, 1) // GROUP
    parts = jnp.where(group == 0, high, jnp.where(group == 1, middle, rest - middle))
    return parts.astype(wire)


def join_logs(parts):
    parts = parts.astype(jnp.float32)
    return parts + pltpu.roll(parts, LANES - GROUP, 1) + pltpu.roll(parts, LANES - 2 * GROUP, 1)


def unit_kernel(listed, merging, chunk, ids_ref, lens_ref, sizes_ref, base_ref, *refs):
    q_refs, refs = refs[:listed], refs[listed:]
    k_ref, v_ref, refs = refs[0], refs[1], refs[2:]
    r_ref, refs = (refs[0], refs[1:]) if merging else (None, refs)
    o_ref, q_ref, p_ref, x_ref, a_ref, f_ref, t_ref, h_ref, g_ref, m_ref = refs
    unit = pl.program_id(0)
    request = ids_ref[unit]
    block = k_ref.shape[1]
    node_count = q_ref.shape[0]
    live = jnp.clip(lens_ref[request] - base_ref[0], 0, block)
    tiles = (sizes_ref[request] + NODES - 1) // NODES
    step = 256
    part = min(block, 512)
    part_chunks = (live + part - 1) // part
    whole_chunks = live // chunk

    def score(queries, at, width):
        return lax.dot_general(
            queries,
            k_ref[0, pl.ds(at, width), :],
            (((1,), (1,)), ((), ())),
            preferred_element_type=jnp.float32,
        )

    def weigh(scores):
        return [
            jnp.exp2(scores[:, i : i + LANES] * exp2_scale - h_ref[...]).astype(jnp.bfloat16)
            for i in range(0, scores.shape[1], LANES)
        ]

    def masked(scores, at):
        column = lax.broadcasted_iota(jnp.int32, scores.shape, 1)
        return jnp.where(column < live - at, scores, negative_fill)

    def shift_of(best):
        peaks = jnp.max(best, axis=1, keepdims=True) * exp2_scale
        return jnp.broadcast_to(peaks, best.shape)

    def take(t):
        start = pl.multiple_of(t * NODES, NODES)
        return jnp.concatenate(
            [q_ref[pl.ds(start, NODES), h * HD : (h + 1) * HD] for h in range(GROUP)], axis=0
        )

    def sample(t):
        queries = take(t)
        return queries, shift_of(masked(score(queries, 0, LANES), 0))

    def chunk_sums(at, place):
        for i in range(0, chunk, step):
            for j, piece in enumerate(weigh(score(t_ref[...], at + i, step))):
                p_ref[:, place + i + j * LANES : place + i + (j + 1) * LANES] = piece
        return jnp.dot(
            p_ref[:, place : place + chunk], x_ref[pl.ds(at, chunk), :], preferred_element_type=jnp.float32
        )

    def whole_block():
        chunks = block // chunk
        for c in range(chunks):
            sums = chunk_sums(c * chunk, c * chunk)
            if c > 0:
                sums = a_ref[...] + sums
            if c < chunks - 1:
                a_ref[...] = sums
            else:
                f_ref[...] = sums

    def part_block():
        f_ref[...] = jnp.zeros(f_ref.shape, jnp.float32)

        @pl.loop(0, whole_chunks)
        def _(c):
            f_ref[...] += chunk_sums(pl.multiple_of(c * chunk, chunk), 0)

        @pl.loop(whole_chunks * (chunk // part), part_chunks)
        def _(c):
            at = pl.multiple_of(c * part, part)
            weights = jnp.concatenate(weigh(masked(score(t_ref[...], at, part), at)), axis=1)
            f_ref[...] += jnp.dot(weights, x_ref[pl.ds(at, part), :], preferred_element_type=jnp.float32)

    def exact_shift():
        g_ref[...] = jnp.full(g_ref.shape, negative_fill, jnp.float32)

        @pl.loop(0, part_chunks)
        def _(c):
            at = pl.multiple_of(c * part, part)
            best = lane_max(masked(score(t_ref[...], at, part), at))
            g_ref[...] = jnp.maximum(g_ref[...], best)

        h_ref[...] = shift_of(g_ref[...])

    def finish(t):
        rows = pl.ds(pl.multiple_of(jnp.maximum(t, 0) * NODES, NODES), NODES)
        totals = f_ref[:, LANES:]
        m_ref[...] = jnp.maximum(m_ref[...], jnp.where(t >= 0, totals, 0.0))
        inverse = 1.0 / totals
        logs = g_ref[...] * math.log(2.0) + jnp.log(totals)
        other_logs = join_logs(r_ref[0, rows, WIDE:]) if merging else None
        head_logs = []
        for h in range(GROUP):
            at = slice(h * NODES, (h + 1) * NODES)
            columns = slice(h * HD, (h + 1) * HD)
            partial = f_ref[at, :LANES] * inverse[at]
            log = logs[at]
            if merging:
                other = jnp.broadcast_to(other_logs[:, h : h + 1], (NODES, LANES))
                top = jnp.maximum(log, other)
                own_weight = jnp.exp(log - top)
                other_weight = jnp.exp(other - top)
                total = own_weight + other_weight
                mixed = partial * own_weight + r_ref[0, rows, columns].astype(jnp.float32) * other_weight
                partial = mixed / total
                log = top + jnp.log(total)
            o_ref[0, rows, columns] = partial.astype(wire)
            head_logs.append(log)
        o_ref[0, rows, WIDE:] = split_logs(place_logs(head_logs))

    @pl.when(unit == 0)
    def _():
        x_ref[:, HD:] = jnp.ones((block, LANES), x_ref.dtype)

    @pl.when(live == 0)
    def _():
        if merging:
            o_ref[...] = r_ref[...]
        else:
            o_ref[0, :, :WIDE] = jnp.zeros((node_count, WIDE), wire)
            o_ref[0, :, WIDE:] = split_logs(jnp.full((node_count, LANES), negative_fill, jnp.float32))

    @pl.when(live > 0)
    def _():
        if listed == 1:
            q_ref[...] = q_refs[0][...]
        else:
            for i in range(listed):

                @pl.when(unit == i)
                def _():
                    q_ref[...] = q_refs[i][...]

        x_ref[:, :HD] = v_ref[0]
        m_ref[...] = jnp.zeros(m_ref.shape, jnp.float32)

    @pl.when(live == block)
    def _():
        queries, shift = sample(0)
        t_ref[...] = queries
        h_ref[...] = shift

        @pl.loop(0, tiles)
        def _(t):
            finish(t - 1)
            g_ref[...] = h_ref[...]
            queries, shift = sample(jnp.minimum(t + 1, tiles - 1))
            whole_block()
            t_ref[...] = queries
            h_ref[...] = shift

        finish(tiles - 1)

    @pl.loop(0, 2)
    def _(exact):
        overflowed = jnp.logical_not(jnp.max(m_ref[...]) < 2.0**100)
        first = jnp.logical_and(exact == 0, live < block)
        again = jnp.logical_and(exact == 1, overflowed)

        @pl.when(jnp.logical_and(live > 0, jnp.logical_or(first, again)))
        def _():
            @pl.loop(0, tiles)
            def _(t):
                t_ref[...] = take(t)

                @pl.when(exact == 0)
                def _():
                    h_ref[...] = shift_of(masked(score(t_ref[...], 0, LANES), 0))

                @pl.when(exact == 1)
                def _():
                    exact_shift()

                part_block()
                g_ref[...] = h_ref[...]
                finish(t)


def unit_attention(queries, ids, kv_head, cache_keys, cache_values, lens, sizes, base, node_count, received=None):
    units = ids.shape[0] // 2
    block = cache_keys.shape[1]
    chunk = min(block, 1024)
    merging = received is not None
    width = WIDE + LANES

    def cache_map(u, ids_ref, *_):
        return (ids_ref[u], 0, kv_head)

    def unit_map(u, *_):
        return (u, 0, 0)

    def received_map(u, ids_ref, *_):
        return (ids_ref[2 * units] + u, 0, 0)

    if isinstance(queries, list):
        in_specs = [
            pl.BlockSpec((node_count, WIDE), functools.partial(lambda i, u, ids_ref, *_: (ids_ref[units + i], 0), i))
            for i in range(units)
        ]
    else:
        queries = [queries]
        in_specs = [pl.BlockSpec((node_count, WIDE), lambda u, ids_ref, *_: (ids_ref[units + u], 0))]
    operands = queries + [cache_keys, cache_values]
    in_specs = in_specs + [pl.BlockSpec((1, block, HD), cache_map)] * 2
    if merging:
        in_specs.append(pl.BlockSpec((1, node_count, width), received_map))
        operands.append(received)
    grid_spec = pltpu.PrefetchScalarGridSpec(
        num_scalar_prefetch=4,
        grid=(units,),
        in_specs=in_specs,
        out_specs=pl.BlockSpec((1, node_count, width), unit_map),
        scratch_shapes=[
            pltpu.VMEM((node_count, WIDE), jnp.bfloat16),
            pltpu.VMEM((ROWS, block), jnp.bfloat16),
            pltpu.VMEM((block, 2 * LANES), jnp.bfloat16),
            pltpu.VMEM((ROWS, 2 * LANES), jnp.float32),
            pltpu.VMEM((ROWS, 2 * LANES), jnp.float32),
            pltpu.VMEM((ROWS, HD), jnp.bfloat16),
            pltpu.VMEM((ROWS, LANES), jnp.float32),
            pltpu.VMEM((ROWS, LANES), jnp.float32),
            pltpu.VMEM((ROWS, LANES), jnp.float32),
        ],
    )
    return pl.pallas_call(
        functools.partial(unit_kernel, len(queries), merging, chunk),
        grid_spec=grid_spec,
        out_shape=jax.ShapeDtypeStruct((units, node_count, width), wire),
        compiler_params=pltpu.CompilerParams(vmem_limit_bytes=48 * 1024 * 1024),
        cost_estimate=pl.CostEstimate(
            flops=4 * units * node_count * GROUP * block * HD,
            bytes_accessed=units * (4 * block * HD + 4 * node_count * width),
            transcendentals=units * node_count * GROUP * block,
        ),
    )(ids, lens, sizes, base, *operands)


def tree_kernel(first_ref, *refs):
    kv_local = len(refs) - 6
    q_refs = refs[:kv_local]
    k_ref, v_ref, parents_ref, o_ref, l_ref, r_ref = refs[kv_local:]
    rows_owned = q_refs[0].shape[0]
    node_count = k_ref.shape[0]
    steps = (node_count - 1).bit_length()
    node = lax.broadcasted_iota(jnp.int32, (node_count, node_count), 0)
    other = lax.broadcasted_iota(jnp.int32, (node_count, node_count), 1)
    linked = jnp.logical_or(parents_ref[...] == node, node == other)
    reached = linked.astype(jnp.float32)
    for _ in range(steps):
        half = reached.astype(jnp.bfloat16)
        reached = jnp.minimum(jnp.dot(half, half, preferred_element_type=jnp.float32), 1.0)
    r_ref[...] = reached.T
    tile = min(rows_owned, NODES)
    for g in range(kv_local):
        keys = k_ref[:, g * HD : (g + 1) * HD]
        values = v_ref[:, g * HD : (g + 1) * HD]

        @pl.loop(0, rows_owned // tile)
        def _(t):
            start = pl.multiple_of(t * tile, tile)
            first = pl.multiple_of(first_ref[0] + start, tile)
            queries = jnp.concatenate(
                [q_refs[g][pl.ds(start, tile), h * HD : (h + 1) * HD] for h in range(GROUP)], axis=0
            )
            live = jnp.concatenate([r_ref[pl.ds(first, tile), :]] * GROUP, axis=0) > 0.5
            scores = lax.dot_general(
                queries, keys, (((1,), (1,)), ((), ())), preferred_element_type=jnp.float32
            )
            scores = jnp.where(live, scores, negative_fill)
            peaks = jnp.max(scores, axis=1, keepdims=True)
            weights = jnp.where(live, jnp.exp2((scores - peaks) * exp2_scale), 0.0)
            totals = jnp.maximum(jnp.sum(weights, axis=1, keepdims=True), 1.0)
            sums = jnp.dot(weights.astype(jnp.bfloat16), values, preferred_element_type=jnp.float32)
            partials = sums / totals
            for h in range(GROUP):
                o_ref[g, pl.ds(start, tile), h * HD : (h + 1) * HD] = partials[h * tile : (h + 1) * tile, :]
            logs = jnp.broadcast_to(peaks * softmax_scale + jnp.log(totals), (GROUP * tile, LANES))
            l_ref[g, pl.ds(start, tile), :] = place_logs([logs[h * tile : (h + 1) * tile] for h in range(GROUP)])


def tree_attention(queries, keys, values, parents, first):
    rows = queries[0].shape[0]
    node_count = keys.shape[0]
    kv_local = len(queries)
    vmem = pl.BlockSpec(memory_space=pltpu.VMEM)
    return pl.pallas_call(
        tree_kernel,
        in_specs=[pl.BlockSpec(memory_space=pltpu.SMEM)] + [vmem] * (kv_local + 3),
        out_specs=[vmem, vmem],
        out_shape=[
            jax.ShapeDtypeStruct((kv_local, rows, WIDE), jnp.float32),
            jax.ShapeDtypeStruct((kv_local, rows, LANES), jnp.float32),
        ],
        scratch_shapes=[pltpu.VMEM((node_count, node_count), jnp.float32)],
        compiler_params=pltpu.CompilerParams(vmem_limit_bytes=32 * 1024 * 1024),
        cost_estimate=pl.CostEstimate(flops=10**9, bytes_accessed=10**7, transcendentals=10**6),
    )(first, *queries, keys, values, parents)


def merge_kernel(parts, alive_ref, *refs):
    kv_local = len(parts)
    o_ref = refs[-1]
    tree_ref, tree_logs_ref = refs[-3], refs[-2]
    rows = o_ref.shape[0]
    lane = lax.broadcasted_iota(jnp.int32, (LANES, WIDE), 0)
    head = lax.broadcasted_iota(jnp.int32, (LANES, WIDE), 1) // HD
    spread = jnp.logical_and(lane % GROUP == head, lane < 3 * GROUP).astype(jnp.bfloat16)
    group = lax.broadcasted_iota(jnp.int32, (rows, LANES), 1) // GROUP
    at_part = 0
    for g in range(kv_local):
        part_refs = refs[at_part : at_part + parts[g]]
        at_part += parts[g]
        logs = [join_logs(ref[0, :, WIDE:]) for ref in part_refs] + [tree_logs_ref[g]]
        top = functools.reduce(jnp.maximum, logs)
        weights = [jnp.exp(log - top) for log in logs]
        scale = 1.0 / functools.reduce(jnp.add, weights)
        total = None
        for j, weight in enumerate(weights):
            share = jnp.where(group == 0, weight * scale, 0.0)
            share = share + pltpu.roll(share, GROUP, 1) + pltpu.roll(share, 2 * GROUP, 1)
            wide = jnp.dot(split_logs(share), spread, preferred_element_type=jnp.float32)
            piece = tree_ref[g] if j == parts[g] else part_refs[j][0, :, :WIDE].astype(jnp.float32)
            total = wide * piece if total is None else total + wide * piece
        alive = alive_ref[:, :1] > 0.5
        o_ref[:, g * WIDE : (g + 1) * WIDE] = jnp.where(alive, total, 0.0).astype(o_ref.dtype)


def merge(parts, tree_partials, tree_logs, alive):
    kv_local, rows, _ = tree_partials.shape
    tile = min(rows, NODES)
    flat = [pair for of_head in parts for pair in of_head]
    return pl.pallas_call(
        functools.partial(merge_kernel, [len(of_head) for of_head in parts]),
        grid=(rows // tile,),
        in_specs=[pl.BlockSpec((tile, LANES), lambda i: (i, 0))]
        + [
            pl.BlockSpec((1, tile, WIDE + LANES), functools.partial(lambda u, i: (u, i, 0), unit))
            for _, unit in flat
        ]
        + [
            pl.BlockSpec((kv_local, tile, WIDE), lambda i: (0, i, 0)),
            pl.BlockSpec((kv_local, tile, LANES), lambda i: (0, i, 0)),
        ],
        out_specs=pl.BlockSpec((tile, kv_local * WIDE), lambda i: (i, 0)),
        out_shape=jax.ShapeDtypeStruct((rows, kv_local * WIDE), jnp.bfloat16),
        compiler_params=pltpu.CompilerParams(vmem_limit_bytes=48 * 1024 * 1024),
    )(alive, *[array for array, _ in flat], tree_partials, tree_logs)


def exchange(array, distance):
    owners = lax.axis_size("req")
    return lax.ppermute(array, "req", [(r, r ^ distance) for r in range(owners)])


def body(
    queries, cache_keys, cache_values, tree_keys, tree_values, parents, tree_sizes, cache_lens
):
    owner_index = lax.axis_index("req")
    owners = lax.axis_size("req")
    requests = cache_keys.shape[0]
    block = cache_keys.shape[1]
    kv_local = cache_keys.shape[2] // HD
    node_count = parents.shape[1]
    rows_owned = tree_keys.shape[0]
    head_devices = lax.axis_size("head")
    own = []
    for g in range(kv_local):
        columns = [
            queries[:, (d * kv_local + g) * WIDE : (d * kv_local + g + 1) * WIDE] for d in range(head_devices)
        ]
        mine = jnp.concatenate(columns, axis=1) if kv_local > 1 else queries
        own.append(lax.all_to_all(mine, "head", split_axis=1, concat_axis=0, tiled=True))

    first_row = owner_index * rows_owned
    request = first_row // node_count
    first_node = first_row % node_count
    if rows_owned < node_count:
        every_key = lax.all_gather(tree_keys, "req", axis=0, tiled=True)
        every_value = lax.all_gather(tree_values, "req", axis=0, tiled=True)
        own_keys = lax.dynamic_slice_in_dim(every_key, request * node_count, node_count, 0)
        own_values = lax.dynamic_slice_in_dim(every_value, request * node_count, node_count, 0)
    else:
        own_keys, own_values = tree_keys, tree_values
    own_parents = lax.dynamic_slice_in_dim(parents, request, 1, 0)

    def attend_tree(after=None):
        first = first_node[None]
        if after is not None:
            first, _ = lax.optimization_barrier((first, after))
        return tree_attention(own, own_keys, own_values, own_parents, first)

    size = lax.dynamic_index_in_dim(tree_sizes, request, 0, keepdims=False)
    alive = first_node + jnp.arange(rows_owned, dtype=jnp.int32) < size
    alive = jnp.broadcast_to(alive[:, None].astype(jnp.float32), (rows_owned, LANES))
    base = (owner_index * block)[None]

    def attend(queries, targets, blocks, kv_head, received=None, offset=0, after=None):
        ids = jnp.stack([jnp.asarray(i, jnp.int32) for i in [*targets, *blocks, offset]])
        if after is not None:
            ids, _ = lax.optimization_barrier((ids, after))
        return unit_attention(
            queries, ids, kv_head, cache_keys, cache_values, cache_lens, tree_sizes, base, node_count, received
        )

    if owners == 8 and rows_owned == node_count and kv_local == 2:
        r = owner_index
        core = r % 2
        cores = [[2 * i, 2 * i + 1] for i in range(4)]
        ours, theirs = [r ^ 2, r ^ 4, r ^ 6], [r ^ 3, r ^ 5, r ^ 7]

        def gather(array):
            return lax.all_gather(array, "req", axis=0, tiled=True, axis_index_groups=cores)

        def send(partials):
            return [exchange(partials[i : i + 1], 2 * (i + 1) + 1) for i in range(3)]

        sibling = exchange(own[0], 1)
        first = [exchange(own[0], distance) for distance in (2, 4, 6)]
        near0 = attend([own[0], sibling], [r, r ^ 1], [0, 0], 0)
        from_near0 = exchange(near0[1:2], 1)
        tree_partials, tree_logs = attend_tree((near0, first))
        shared, _ = lax.optimization_barrier((first, tree_logs))
        first_all = [gather(q) for q in shared]
        late, _ = lax.optimization_barrier((own[1], tree_logs))
        second = [exchange(late, distance) for distance in (2, 4, 6)]
        sibling1 = exchange(late, 1)
        ours0 = attend(first, ours, [0, 0, 0], 0, after=(tree_logs, from_near0))
        swapped0 = gather(ours0)
        ours1 = attend(second, ours, [0, 0, 0], 1, after=ours0)
        shared1, _ = lax.optimization_barrier((second, ours1))
        second_all = [gather(q) for q in shared1]
        swapped1 = gather(ours1)
        sibling_part = 3 * (1 - core)
        theirs0 = attend(first_all, theirs, [1 - core] * 3, 0, swapped0, sibling_part, after=ours1)
        sent0 = send(theirs0)
        theirs1 = attend(second_all, theirs, [1 - core] * 3, 1, swapped1, sibling_part, after=theirs0)
        sent1 = send(theirs1)
        near1 = attend([own[1], sibling1], [r, r ^ 1], [0, 0], 1, after=(theirs1, sent0))
        from_near1 = exchange(near1[1:2], 1)
        parts = [
            [(near0, 0), (from_near0, 0)] + [(piece, 0) for piece in sent0],
            [(near1, 0), (from_near1, 0)] + [(piece, 0) for piece in sent1],
        ]
        return merge(parts, tree_partials, tree_logs, alive)

    tree_partials, tree_logs = attend_tree()
    every = [lax.all_gather(q, "req", axis=0, tiled=True) for q in own]
    targets = list(range(requests))
    partials = jnp.stack([attend(every[g], targets, targets, g) for g in range(kv_local)])
    partials = partials.reshape(kv_local, owners, rows_owned, WIDE + LANES)
    partials = lax.all_to_all(partials, "req", split_axis=1, concat_axis=1)
    partials = partials.reshape(kv_local * owners, rows_owned, WIDE + LANES)
    parts = [[(partials, g * owners + j) for j in range(owners)] for g in range(kv_local)]
    return merge(parts, tree_partials, tree_logs, alive)


def solution(mesh):
    placed = (
        P(("req", "head"), None),
        P(None, "req", "head"),
        P(None, "req", "head"),
        P("req", "head"),
        P("req", "head"),
        P(),
        P(),
        P(),
    )
    return jax.shard_map(
        body, mesh=mesh, in_specs=placed, out_specs=P("req", "head"), check_vma=False
    )
```

```python
import functools
import math

import jax
import jax.numpy as jnp
from jax import lax
from jax.experimental import pallas as pl
from jax.experimental.pallas import tpu as pltpu
from jax.sharding import PartitionSpec as P

NH = 128
KVH = 8
HD = 128
GROUP = NH // KVH
WIDE = GROUP * HD
LANES = 128
NODES = 32
ROWS = GROUP * NODES

negative_fill = -1e30
softmax_scale = 1.0 / math.sqrt(HD)
exp2_scale = softmax_scale * math.log2(math.e)
wire = jnp.bfloat16


def lane_max(scores):
    best = scores[:, :LANES]
    for at in range(LANES, scores.shape[1], LANES):
        best = jnp.maximum(best, scores[:, at : at + LANES])
    return best


def place_logs(logs):
    lane = lax.broadcasted_iota(jnp.int32, logs[0].shape, 1) % GROUP
    placed = logs[0]
    for head in range(1, GROUP):
        placed = jnp.where(lane == head, logs[head], placed)
    return placed


def split_logs(logs):
    high = logs.astype(wire).astype(jnp.float32)
    rest = logs - high
    middle = rest.astype(wire).astype(jnp.float32)
    group = lax.broadcasted_iota(jnp.int32, logs.shape, 1) // GROUP
    parts = jnp.where(group == 0, high, jnp.where(group == 1, middle, rest - middle))
    return parts.astype(wire)


def join_logs(parts):
    parts = parts.astype(jnp.float32)
    return parts + pltpu.roll(parts, LANES - GROUP, 1) + pltpu.roll(parts, LANES - 2 * GROUP, 1)


def unit_kernel(listed, merging, chunk, ids_ref, lens_ref, sizes_ref, base_ref, *refs):
    q_refs, refs = refs[:listed], refs[listed:]
    k_ref, v_ref, refs = refs[0], refs[1], refs[2:]
    r_ref, refs = (refs[0], refs[1:]) if merging else (None, refs)
    o_ref, q_ref, p_ref, x_ref, a_ref, f_ref, t_ref, h_ref, g_ref, m_ref = refs
    unit = pl.program_id(0)
    request = ids_ref[unit]
    block = k_ref.shape[1]
    node_count = q_ref.shape[0]
    live = jnp.clip(lens_ref[request] - base_ref[0], 0, block)
    tiles = (sizes_ref[request] + NODES - 1) // NODES
    step = 256
    part = min(block, 512)
    part_chunks = (live + part - 1) // part
    whole_chunks = live // chunk

    def score(queries, at, width):
        return lax.dot_general(
            queries,
            k_ref[0, pl.ds(at, width), :],
            (((1,), (1,)), ((), ())),
            preferred_element_type=jnp.float32,
        )

    def weigh(scores):
        return [
            jnp.exp2(scores[:, i : i + LANES] * exp2_scale - h_ref[...]).astype(jnp.bfloat16)
            for i in range(0, scores.shape[1], LANES)
        ]

    def masked(scores, at):
        column = lax.broadcasted_iota(jnp.int32, scores.shape, 1)
        return jnp.where(column < live - at, scores, negative_fill)

    def shift_of(best):
        peaks = jnp.max(best, axis=1, keepdims=True) * exp2_scale
        return jnp.broadcast_to(peaks, best.shape)

    def take(t):
        start = pl.multiple_of(t * NODES, NODES)
        return jnp.concatenate(
            [q_ref[pl.ds(start, NODES), h * HD : (h + 1) * HD] for h in range(GROUP)], axis=0
        )

    def sample(t):
        queries = take(t)
        return queries, shift_of(masked(score(queries, 0, LANES), 0))

    def chunk_sums(at, place):
        for i in range(0, chunk, step):
            for j, piece in enumerate(weigh(score(t_ref[...], at + i, step))):
                p_ref[:, place + i + j * LANES : place + i + (j + 1) * LANES] = piece
        return jnp.dot(
            p_ref[:, place : place + chunk], x_ref[pl.ds(at, chunk), :], preferred_element_type=jnp.float32
        )

    def whole_block():
        chunks = block // chunk
        for c in range(chunks):
            sums = chunk_sums(c * chunk, c * chunk)
            if c > 0:
                sums = a_ref[...] + sums
            if c < chunks - 1:
                a_ref[...] = sums
            else:
                f_ref[...] = sums

    def part_block():
        f_ref[...] = jnp.zeros(f_ref.shape, jnp.float32)

        @pl.loop(0, whole_chunks)
        def _(c):
            f_ref[...] += chunk_sums(pl.multiple_of(c * chunk, chunk), 0)

        @pl.loop(whole_chunks * (chunk // part), part_chunks)
        def _(c):
            at = pl.multiple_of(c * part, part)
            weights = jnp.concatenate(weigh(masked(score(t_ref[...], at, part), at)), axis=1)
            f_ref[...] += jnp.dot(weights, x_ref[pl.ds(at, part), :], preferred_element_type=jnp.float32)

    def exact_shift():
        g_ref[...] = jnp.full(g_ref.shape, negative_fill, jnp.float32)

        @pl.loop(0, part_chunks)
        def _(c):
            at = pl.multiple_of(c * part, part)
            best = lane_max(masked(score(t_ref[...], at, part), at))
            g_ref[...] = jnp.maximum(g_ref[...], best)

        h_ref[...] = shift_of(g_ref[...])

    def finish(t):
        rows = pl.ds(pl.multiple_of(jnp.maximum(t, 0) * NODES, NODES), NODES)
        totals = f_ref[:, LANES:]
        m_ref[...] = jnp.maximum(m_ref[...], jnp.where(t >= 0, totals, 0.0))
        inverse = 1.0 / totals
        logs = g_ref[...] * math.log(2.0) + jnp.log(totals)
        other_logs = join_logs(r_ref[0, rows, WIDE:]) if merging else None
        head_logs = []
        for h in range(GROUP):
            at = slice(h * NODES, (h + 1) * NODES)
            columns = slice(h * HD, (h + 1) * HD)
            partial = f_ref[at, :LANES] * inverse[at]
            log = logs[at]
            if merging:
                other = jnp.broadcast_to(other_logs[:, h : h + 1], (NODES, LANES))
                top = jnp.maximum(log, other)
                own_weight = jnp.exp(log - top)
                other_weight = jnp.exp(other - top)
                total = own_weight + other_weight
                mixed = partial * own_weight + r_ref[0, rows, columns].astype(jnp.float32) * other_weight
                partial = mixed / total
                log = top + jnp.log(total)
            o_ref[0, rows, columns] = partial.astype(wire)
            head_logs.append(log)
        o_ref[0, rows, WIDE:] = split_logs(place_logs(head_logs))

    @pl.when(unit == 0)
    def _():
        x_ref[:, HD:] = jnp.ones((block, LANES), x_ref.dtype)

    @pl.when(live == 0)
    def _():
        if merging:
            o_ref[...] = r_ref[...]
        else:
            o_ref[0, :, :WIDE] = jnp.zeros((node_count, WIDE), wire)
            o_ref[0, :, WIDE:] = split_logs(jnp.full((node_count, LANES), negative_fill, jnp.float32))

    @pl.when(live > 0)
    def _():
        if listed == 1:
            q_ref[...] = q_refs[0][...]
        else:
            for i in range(listed):

                @pl.when(unit == i)
                def _():
                    q_ref[...] = q_refs[i][...]

        x_ref[:, :HD] = v_ref[0]
        m_ref[...] = jnp.zeros(m_ref.shape, jnp.float32)

    @pl.when(live == block)
    def _():
        queries, shift = sample(0)
        t_ref[...] = queries
        h_ref[...] = shift

        @pl.loop(0, tiles)
        def _(t):
            finish(t - 1)
            g_ref[...] = h_ref[...]
            queries, shift = sample(jnp.minimum(t + 1, tiles - 1))
            whole_block()
            t_ref[...] = queries
            h_ref[...] = shift

        finish(tiles - 1)

    @pl.loop(0, 2)
    def _(exact):
        overflowed = jnp.logical_not(jnp.max(m_ref[...]) < 2.0**100)
        first = jnp.logical_and(exact == 0, live < block)
        again = jnp.logical_and(exact == 1, overflowed)

        @pl.when(jnp.logical_and(live > 0, jnp.logical_or(first, again)))
        def _():
            @pl.loop(0, tiles)
            def _(t):
                t_ref[...] = take(t)

                @pl.when(exact == 0)
                def _():
                    h_ref[...] = shift_of(masked(score(t_ref[...], 0, LANES), 0))

                @pl.when(exact == 1)
                def _():
                    exact_shift()

                part_block()
                g_ref[...] = h_ref[...]
                finish(t)


def unit_attention(queries, ids, kv_head, cache_keys, cache_values, lens, sizes, base, node_count, received=None):
    units = ids.shape[0] // 2
    block = cache_keys.shape[1]
    chunk = min(block, 1024)
    merging = received is not None
    width = WIDE + LANES

    def cache_map(u, ids_ref, *_):
        return (ids_ref[u], 0, kv_head)

    def unit_map(u, *_):
        return (u, 0, 0)

    def received_map(u, ids_ref, *_):
        return (ids_ref[2 * units] + u, 0, 0)

    if isinstance(queries, list):
        in_specs = [
            pl.BlockSpec((node_count, WIDE), functools.partial(lambda i, u, ids_ref, *_: (ids_ref[units + i], 0), i))
            for i in range(units)
        ]
    else:
        queries = [queries]
        in_specs = [pl.BlockSpec((node_count, WIDE), lambda u, ids_ref, *_: (ids_ref[units + u], 0))]
    operands = queries + [cache_keys, cache_values]
    in_specs = in_specs + [pl.BlockSpec((1, block, HD), cache_map)] * 2
    if merging:
        in_specs.append(pl.BlockSpec((1, node_count, width), received_map))
        operands.append(received)
    grid_spec = pltpu.PrefetchScalarGridSpec(
        num_scalar_prefetch=4,
        grid=(units,),
        in_specs=in_specs,
        out_specs=pl.BlockSpec((1, node_count, width), unit_map),
        scratch_shapes=[
            pltpu.VMEM((node_count, WIDE), jnp.bfloat16),
            pltpu.VMEM((ROWS, block), jnp.bfloat16),
            pltpu.VMEM((block, 2 * LANES), jnp.bfloat16),
            pltpu.VMEM((ROWS, 2 * LANES), jnp.float32),
            pltpu.VMEM((ROWS, 2 * LANES), jnp.float32),
            pltpu.VMEM((ROWS, HD), jnp.bfloat16),
            pltpu.VMEM((ROWS, LANES), jnp.float32),
            pltpu.VMEM((ROWS, LANES), jnp.float32),
            pltpu.VMEM((ROWS, LANES), jnp.float32),
        ],
    )
    return pl.pallas_call(
        functools.partial(unit_kernel, len(queries), merging, chunk),
        grid_spec=grid_spec,
        out_shape=jax.ShapeDtypeStruct((units, node_count, width), wire),
        compiler_params=pltpu.CompilerParams(vmem_limit_bytes=60 * 1024 * 1024),
        cost_estimate=pl.CostEstimate(
            flops=4 * units * node_count * GROUP * block * HD,
            bytes_accessed=units * (4 * block * HD + 4 * node_count * width),
            transcendentals=units * node_count * GROUP * block,
        ),
    )(ids, lens, sizes, base, *operands)


def tree_kernel(first_ref, *refs):
    kv_local = len(refs) - 6
    q_refs = refs[:kv_local]
    k_ref, v_ref, parents_ref, o_ref, l_ref, r_ref = refs[kv_local:]
    rows_owned = q_refs[0].shape[0]
    node_count = k_ref.shape[0]
    steps = (node_count - 1).bit_length()
    node = lax.broadcasted_iota(jnp.int32, (node_count, node_count), 0)
    other = lax.broadcasted_iota(jnp.int32, (node_count, node_count), 1)
    linked = jnp.logical_or(parents_ref[...] == node, node == other)
    reached = linked.astype(jnp.float32)
    for _ in range(steps):
        half = reached.astype(jnp.bfloat16)
        reached = jnp.minimum(jnp.dot(half, half, preferred_element_type=jnp.float32), 1.0)
    r_ref[...] = reached.T
    tile = min(rows_owned, NODES)
    for g in range(kv_local):
        keys = k_ref[:, g * HD : (g + 1) * HD]
        values = v_ref[:, g * HD : (g + 1) * HD]

        @pl.loop(0, jnp.clip((first_ref[1] - first_ref[0] + tile - 1) // tile, 0, rows_owned // tile))
        def _(t):
            start = pl.multiple_of(t * tile, tile)
            first = pl.multiple_of(first_ref[0] + start, tile)
            queries = jnp.concatenate(
                [q_refs[g][pl.ds(start, tile), h * HD : (h + 1) * HD] for h in range(GROUP)], axis=0
            )
            live = jnp.concatenate([r_ref[pl.ds(first, tile), :]] * GROUP, axis=0) > 0.5
            scores = lax.dot_general(
                queries, keys, (((1,), (1,)), ((), ())), preferred_element_type=jnp.float32
            )
            scores = jnp.where(live, scores, negative_fill)
            peaks = jnp.max(scores, axis=1, keepdims=True)
            weights = jnp.where(live, jnp.exp2((scores - peaks) * exp2_scale), 0.0)
            totals = jnp.maximum(jnp.sum(weights, axis=1, keepdims=True), 1.0)
            sums = jnp.dot(weights.astype(jnp.bfloat16), values, preferred_element_type=jnp.float32)
            partials = sums / totals
            for h in range(GROUP):
                o_ref[g, pl.ds(start, tile), h * HD : (h + 1) * HD] = partials[h * tile : (h + 1) * tile, :]
            logs = jnp.broadcast_to(peaks * softmax_scale + jnp.log(totals), (GROUP * tile, LANES))
            l_ref[g, pl.ds(start, tile), :] = place_logs([logs[h * tile : (h + 1) * tile] for h in range(GROUP)])


def tree_attention(queries, keys, values, parents, first):
    rows = queries[0].shape[0]
    node_count = keys.shape[0]
    kv_local = len(queries)
    vmem = pl.BlockSpec(memory_space=pltpu.VMEM)
    return pl.pallas_call(
        tree_kernel,
        in_specs=[pl.BlockSpec(memory_space=pltpu.SMEM)] + [vmem] * (kv_local + 3),
        out_specs=[vmem, vmem],
        out_shape=[
            jax.ShapeDtypeStruct((kv_local, rows, WIDE), jnp.float32),
            jax.ShapeDtypeStruct((kv_local, rows, LANES), jnp.float32),
        ],
        scratch_shapes=[pltpu.VMEM((node_count, node_count), jnp.float32)],
        compiler_params=pltpu.CompilerParams(vmem_limit_bytes=60 * 1024 * 1024),
        cost_estimate=pl.CostEstimate(flops=10**9, bytes_accessed=10**7, transcendentals=10**6),
    )(first, *queries, keys, values, parents)


def merge_kernel(parts, alive_ref, *refs):
    kv_local = len(parts)
    o_ref = refs[-1]
    tree_ref, tree_logs_ref = refs[-3], refs[-2]
    rows = o_ref.shape[0]
    lane = lax.broadcasted_iota(jnp.int32, (LANES, WIDE), 0)
    head = lax.broadcasted_iota(jnp.int32, (LANES, WIDE), 1) // HD
    spread = jnp.logical_and(lane % GROUP == head, lane < 3 * GROUP).astype(jnp.bfloat16)
    group = lax.broadcasted_iota(jnp.int32, (rows, LANES), 1) // GROUP
    at_part = 0
    for g in range(kv_local):
        part_refs = refs[at_part : at_part + parts[g]]
        at_part += parts[g]
        logs = [join_logs(ref[0, :, WIDE:]) for ref in part_refs] + [tree_logs_ref[g]]
        top = functools.reduce(jnp.maximum, logs)
        weights = [jnp.exp(log - top) for log in logs]
        scale = 1.0 / functools.reduce(jnp.add, weights)
        total = None
        for j, weight in enumerate(weights):
            share = jnp.where(group == 0, weight * scale, 0.0)
            share = share + pltpu.roll(share, GROUP, 1) + pltpu.roll(share, 2 * GROUP, 1)
            wide = jnp.dot(split_logs(share), spread, preferred_element_type=jnp.float32)
            piece = tree_ref[g] if j == parts[g] else part_refs[j][0, :, :WIDE].astype(jnp.float32)
            total = wide * piece if total is None else total + wide * piece
        alive = alive_ref[:, :1] > 0.5
        o_ref[:, g * WIDE : (g + 1) * WIDE] = jnp.where(alive, total, 0.0).astype(o_ref.dtype)


def merge(parts, tree_partials, tree_logs, alive):
    kv_local, rows, _ = tree_partials.shape
    tile = min(rows, NODES)
    flat = [pair for of_head in parts for pair in of_head]
    return pl.pallas_call(
        functools.partial(merge_kernel, [len(of_head) for of_head in parts]),
        grid=(rows // tile,),
        in_specs=[pl.BlockSpec((tile, LANES), lambda i: (i, 0))]
        + [
            pl.BlockSpec((1, tile, WIDE + LANES), functools.partial(lambda u, i: (u, i, 0), unit))
            for _, unit in flat
        ]
        + [
            pl.BlockSpec((kv_local, tile, WIDE), lambda i: (0, i, 0)),
            pl.BlockSpec((kv_local, tile, LANES), lambda i: (0, i, 0)),
        ],
        out_specs=pl.BlockSpec((tile, kv_local * WIDE), lambda i: (i, 0)),
        out_shape=jax.ShapeDtypeStruct((rows, kv_local * WIDE), jnp.bfloat16),
        compiler_params=pltpu.CompilerParams(vmem_limit_bytes=40 * 1024 * 1024),
    )(alive, *[array for array, _ in flat], tree_partials, tree_logs)


def exchange(array, distance):
    owners = lax.axis_size("req")
    return lax.ppermute(array, "req", [(r, r ^ distance) for r in range(owners)])


def body(
    queries, cache_keys, cache_values, tree_keys, tree_values, parents, tree_sizes, cache_lens
):
    owner_index = lax.axis_index("req")
    owners = lax.axis_size("req")
    requests = cache_keys.shape[0]
    block = cache_keys.shape[1]
    kv_local = cache_keys.shape[2] // HD
    node_count = parents.shape[1]
    rows_owned = tree_keys.shape[0]
    head_devices = lax.axis_size("head")
    own = []
    for g in range(kv_local):
        columns = [
            queries[:, (d * kv_local + g) * WIDE : (d * kv_local + g + 1) * WIDE] for d in range(head_devices)
        ]
        mine = jnp.concatenate(columns, axis=1) if kv_local > 1 else queries
        own.append(lax.all_to_all(mine, "head", split_axis=1, concat_axis=0, tiled=True))

    first_row = owner_index * rows_owned
    request = first_row // node_count
    first_node = first_row % node_count
    if rows_owned < node_count:
        every_key = lax.all_gather(tree_keys, "req", axis=0, tiled=True)
        every_value = lax.all_gather(tree_values, "req", axis=0, tiled=True)
        own_keys = lax.dynamic_slice_in_dim(every_key, request * node_count, node_count, 0)
        own_values = lax.dynamic_slice_in_dim(every_value, request * node_count, node_count, 0)
    else:
        own_keys, own_values = tree_keys, tree_values
    size = lax.dynamic_index_in_dim(tree_sizes, request, 0, keepdims=False)
    own_parents = lax.dynamic_slice_in_dim(parents, request, 1, 0)

    def attend_tree(after=None):
        first = jnp.stack([first_node, size])
        if after is not None:
            first, _ = lax.optimization_barrier((first, after))
        return tree_attention(own, own_keys, own_values, own_parents, first)

    alive = first_node + jnp.arange(rows_owned, dtype=jnp.int32) < size
    alive = jnp.broadcast_to(alive[:, None].astype(jnp.float32), (rows_owned, LANES))
    base = (owner_index * block)[None]

    def attend(queries, targets, blocks, kv_head, received=None, offset=0, after=None):
        ids = jnp.stack([jnp.asarray(i, jnp.int32) for i in [*targets, *blocks, offset]])
        if after is not None:
            ids, _ = lax.optimization_barrier((ids, after))
        return unit_attention(
            queries, ids, kv_head, cache_keys, cache_values, cache_lens, tree_sizes, base, node_count, received
        )

    if owners == 8 and rows_owned == node_count and kv_local == 2:
        r = owner_index
        chip, core = r // 2, r % 2
        cores = [[2 * i, 2 * i + 1] for i in range(4)]
        chips = [[0, 2, 4, 6], [1, 3, 5, 7]]
        ours, theirs = [r ^ 2, r ^ 4, r ^ 6], [r ^ 3, r ^ 5, r ^ 7]
        our_blocks = [chip ^ 1, chip ^ 2, chip ^ 3]
        their_blocks = [4 * (1 - core) + block for block in our_blocks]

        def gather(array, groups):
            return lax.all_gather(array, "req", axis=0, tiled=True, axis_index_groups=groups)

        def send(partials):
            return [exchange(partials[i : i + 1], 2 * (i + 1) + 1) for i in range(3)]

        first = gather(own[0], chips)
        near0 = attend([own[0], exchange(own[0], 1)], [r, r ^ 1], [0, 0], 0)
        first_all = gather(first, cores)
        late, _ = lax.optimization_barrier((own[1], near0))
        second = gather(late, chips)
        second_all = gather(second, cores)
        from_near0 = exchange(near0[1:2], 1)
        tree_partials, tree_logs = attend_tree(near0)
        ours0 = attend(first, ours, our_blocks, 0, after=(tree_logs, from_near0))
        swapped0 = gather(ours0, cores)
        ours1 = attend(second, ours, our_blocks, 1, after=ours0)
        swapped1 = gather(ours1, cores)
        sibling_part = 3 * (1 - core)
        theirs0 = attend(first_all, theirs, their_blocks, 0, swapped0, sibling_part, after=ours1)
        sent0 = send(theirs0)
        theirs1 = attend(second_all, theirs, their_blocks, 1, swapped1, sibling_part, after=theirs0)
        sent1 = send(theirs1)
        near1 = attend(second_all, [r, r ^ 1], [4 * core + chip, 4 * (1 - core) + chip], 1, after=(theirs1, sent0))
        from_near1 = exchange(near1[1:2], 1)
        parts = [
            [(near0, 0), (from_near0, 0)] + [(piece, 0) for piece in sent0],
            [(near1, 0), (from_near1, 0)] + [(piece, 0) for piece in sent1],
        ]
        return merge(parts, tree_partials, tree_logs, alive)

    tree_partials, tree_logs = attend_tree()
    every = [lax.all_gather(q, "req", axis=0, tiled=True) for q in own]
    targets = list(range(requests))
    partials = jnp.stack([attend(every[g], targets, targets, g) for g in range(kv_local)])
    partials = partials.reshape(kv_local, owners, rows_owned, WIDE + LANES)
    partials = lax.all_to_all(partials, "req", split_axis=1, concat_axis=1)
    partials = partials.reshape(kv_local * owners, rows_owned, WIDE + LANES)
    parts = [[(partials, g * owners + j) for j in range(owners)] for g in range(kv_local)]
    return merge(parts, tree_partials, tree_logs, alive)


def solution(mesh):
    placed = (
        P(("req", "head"), None),
        P(None, "req", "head"),
        P(None, "req", "head"),
        P("req", "head"),
        P("req", "head"),
        P(),
        P(),
        P(),
    )
    return jax.shard_map(
        body, mesh=mesh, in_specs=placed, out_specs=P("req", "head"), check_vma=False
    )
```

```python
import functools
import math

import jax
import jax.numpy as jnp
from jax import lax
from jax.experimental import pallas as pl
from jax.experimental.pallas import tpu as pltpu
from jax.sharding import PartitionSpec as P

NH = 128
KVH = 8
HD = 128
GROUP = NH // KVH
WIDE = GROUP * HD
LANES = 128
NODES = 32
ROWS = GROUP * NODES

negative_fill = -1e30
softmax_scale = 1.0 / math.sqrt(HD)
exp2_scale = softmax_scale * math.log2(math.e)
wire = jnp.bfloat16


def lane_max(scores):
    best = scores[:, :LANES]
    for at in range(LANES, scores.shape[1], LANES):
        best = jnp.maximum(best, scores[:, at : at + LANES])
    return best


def place_logs(logs):
    lane = lax.broadcasted_iota(jnp.int32, logs[0].shape, 1) % GROUP
    placed = logs[0]
    for head in range(1, GROUP):
        placed = jnp.where(lane == head, logs[head], placed)
    return placed


def split_logs(logs):
    high = logs.astype(wire).astype(jnp.float32)
    rest = logs - high
    middle = rest.astype(wire).astype(jnp.float32)
    group = lax.broadcasted_iota(jnp.int32, logs.shape, 1) // GROUP
    parts = jnp.where(group == 0, high, jnp.where(group == 1, middle, rest - middle))
    return parts.astype(wire)


def join_logs(parts):
    parts = parts.astype(jnp.float32)
    return parts + pltpu.roll(parts, LANES - GROUP, 1) + pltpu.roll(parts, LANES - 2 * GROUP, 1)


def unit_kernel(listed, merging, chunk, ids_ref, lens_ref, sizes_ref, base_ref, *refs):
    q_refs, refs = refs[:listed], refs[listed:]
    k_ref, v_ref, refs = refs[0], refs[1], refs[2:]
    r_ref, refs = (refs[0], refs[1:]) if merging else (None, refs)
    o_ref, q_ref, p_ref, x_ref, a_ref, f_ref, t_ref, h_ref, g_ref, m_ref = refs
    unit = pl.program_id(0)
    request = ids_ref[unit]
    block = k_ref.shape[1]
    node_count = q_ref.shape[0]
    live = jnp.clip(lens_ref[request] - base_ref[0], 0, block)
    tiles = (sizes_ref[request] + NODES - 1) // NODES
    step = 256
    part = min(block, 512)
    part_chunks = (live + part - 1) // part
    whole_chunks = live // chunk

    def score(queries, at, width):
        return lax.dot_general(
            queries,
            k_ref[0, pl.ds(at, width), :],
            (((1,), (1,)), ((), ())),
            preferred_element_type=jnp.float32,
        )

    def weigh(scores):
        return [
            jnp.exp2(scores[:, i : i + LANES] * exp2_scale - h_ref[...]).astype(jnp.bfloat16)
            for i in range(0, scores.shape[1], LANES)
        ]

    def masked(scores, at):
        column = lax.broadcasted_iota(jnp.int32, scores.shape, 1)
        return jnp.where(column < live - at, scores, negative_fill)

    def shift_of(best):
        peaks = jnp.max(best, axis=1, keepdims=True) * exp2_scale
        return jnp.broadcast_to(peaks, best.shape)

    def take(t):
        start = pl.multiple_of(t * NODES, NODES)
        return jnp.concatenate(
            [q_ref[pl.ds(start, NODES), h * HD : (h + 1) * HD] for h in range(GROUP)], axis=0
        )

    def sample(t):
        queries = take(t)
        return queries, shift_of(masked(score(queries, 0, LANES), 0))

    def chunk_sums(at, place):
        for i in range(0, chunk, step):
            for j, piece in enumerate(weigh(score(t_ref[...], at + i, step))):
                p_ref[:, place + i + j * LANES : place + i + (j + 1) * LANES] = piece
        return jnp.dot(
            p_ref[:, place : place + chunk], x_ref[pl.ds(at, chunk), :], preferred_element_type=jnp.float32
        )

    def whole_block():
        chunks = block // chunk
        for c in range(chunks):
            sums = chunk_sums(c * chunk, c * chunk)
            if c > 0:
                sums = a_ref[...] + sums
            if c < chunks - 1:
                a_ref[...] = sums
            else:
                f_ref[...] = sums

    def part_block():
        f_ref[...] = jnp.zeros(f_ref.shape, jnp.float32)

        @pl.loop(0, whole_chunks)
        def _(c):
            f_ref[...] += chunk_sums(pl.multiple_of(c * chunk, chunk), 0)

        @pl.loop(whole_chunks * (chunk // part), part_chunks)
        def _(c):
            at = pl.multiple_of(c * part, part)
            weights = jnp.concatenate(weigh(masked(score(t_ref[...], at, part), at)), axis=1)
            f_ref[...] += jnp.dot(weights, x_ref[pl.ds(at, part), :], preferred_element_type=jnp.float32)

    def exact_shift():
        g_ref[...] = jnp.full(g_ref.shape, negative_fill, jnp.float32)

        @pl.loop(0, part_chunks)
        def _(c):
            at = pl.multiple_of(c * part, part)
            best = lane_max(masked(score(t_ref[...], at, part), at))
            g_ref[...] = jnp.maximum(g_ref[...], best)

        h_ref[...] = shift_of(g_ref[...])

    def finish(t):
        rows = pl.ds(pl.multiple_of(jnp.maximum(t, 0) * NODES, NODES), NODES)
        totals = f_ref[:, LANES:]
        m_ref[...] = jnp.maximum(m_ref[...], jnp.where(t >= 0, totals, 0.0))
        inverse = 1.0 / totals
        logs = g_ref[...] * math.log(2.0) + jnp.log(totals)
        other_logs = join_logs(r_ref[0, rows, WIDE:]) if merging else None
        head_logs = []
        for h in range(GROUP):
            at = slice(h * NODES, (h + 1) * NODES)
            columns = slice(h * HD, (h + 1) * HD)
            partial = f_ref[at, :LANES] * inverse[at]
            log = logs[at]
            if merging:
                other = jnp.broadcast_to(other_logs[:, h : h + 1], (NODES, LANES))
                top = jnp.maximum(log, other)
                own_weight = jnp.exp(log - top)
                other_weight = jnp.exp(other - top)
                total = own_weight + other_weight
                mixed = partial * own_weight + r_ref[0, rows, columns].astype(jnp.float32) * other_weight
                partial = mixed / total
                log = top + jnp.log(total)
            o_ref[0, rows, columns] = partial.astype(wire)
            head_logs.append(log)
        o_ref[0, rows, WIDE:] = split_logs(place_logs(head_logs))

    @pl.when(unit == 0)
    def _():
        x_ref[:, HD:] = jnp.ones((block, LANES), x_ref.dtype)

    @pl.when(live == 0)
    def _():
        if merging:
            o_ref[...] = r_ref[...]
        else:
            o_ref[0, :, :WIDE] = jnp.zeros((node_count, WIDE), wire)
            o_ref[0, :, WIDE:] = split_logs(jnp.full((node_count, LANES), negative_fill, jnp.float32))

    @pl.when(live > 0)
    def _():
        if listed == 1:
            q_ref[...] = q_refs[0][...]
        else:
            for i in range(listed):

                @pl.when(unit == i)
                def _():
                    q_ref[...] = q_refs[i][...]

        x_ref[:, :HD] = v_ref[0]
        m_ref[...] = jnp.zeros(m_ref.shape, jnp.float32)

    @pl.when(live == block)
    def _():
        queries, shift = sample(0)
        t_ref[...] = queries
        h_ref[...] = shift

        @pl.loop(0, tiles)
        def _(t):
            finish(t - 1)
            g_ref[...] = h_ref[...]
            queries, shift = sample(jnp.minimum(t + 1, tiles - 1))
            whole_block()
            t_ref[...] = queries
            h_ref[...] = shift

        finish(tiles - 1)

    @pl.loop(0, 2)
    def _(exact):
        overflowed = jnp.logical_not(jnp.max(m_ref[...]) < 2.0**100)
        first = jnp.logical_and(exact == 0, live < block)
        again = jnp.logical_and(exact == 1, overflowed)

        @pl.when(jnp.logical_and(live > 0, jnp.logical_or(first, again)))
        def _():
            @pl.loop(0, tiles)
            def _(t):
                t_ref[...] = take(t)

                @pl.when(exact == 0)
                def _():
                    h_ref[...] = shift_of(masked(score(t_ref[...], 0, LANES), 0))

                @pl.when(exact == 1)
                def _():
                    exact_shift()

                part_block()
                g_ref[...] = h_ref[...]
                finish(t)


def unit_attention(queries, ids, kv_head, cache_keys, cache_values, lens, sizes, base, node_count, received=None):
    units = ids.shape[0] // 2
    block = cache_keys.shape[1]
    chunk = min(block, 1024)
    merging = received is not None
    width = WIDE + LANES

    def cache_map(u, ids_ref, *_):
        return (ids_ref[u], 0, kv_head)

    def unit_map(u, *_):
        return (u, 0, 0)

    def received_map(u, ids_ref, *_):
        return (ids_ref[2 * units] + u, 0, 0)

    if isinstance(queries, list):
        in_specs = [
            pl.BlockSpec((node_count, WIDE), functools.partial(lambda i, u, ids_ref, *_: (ids_ref[units + i], 0), i))
            for i in range(units)
        ]
    else:
        queries = [queries]
        in_specs = [pl.BlockSpec((node_count, WIDE), lambda u, ids_ref, *_: (ids_ref[units + u], 0))]
    operands = queries + [cache_keys, cache_values]
    in_specs = in_specs + [pl.BlockSpec((1, block, HD), cache_map)] * 2
    if merging:
        in_specs.append(pl.BlockSpec((1, node_count, width), received_map))
        operands.append(received)
    grid_spec = pltpu.PrefetchScalarGridSpec(
        num_scalar_prefetch=4,
        grid=(units,),
        in_specs=in_specs,
        out_specs=pl.BlockSpec((1, node_count, width), unit_map),
        scratch_shapes=[
            pltpu.VMEM((node_count, WIDE), jnp.bfloat16),
            pltpu.VMEM((ROWS, block), jnp.bfloat16),
            pltpu.VMEM((block, 2 * LANES), jnp.bfloat16),
            pltpu.VMEM((ROWS, 2 * LANES), jnp.float32),
            pltpu.VMEM((ROWS, 2 * LANES), jnp.float32),
            pltpu.VMEM((ROWS, HD), jnp.bfloat16),
            pltpu.VMEM((ROWS, LANES), jnp.float32),
            pltpu.VMEM((ROWS, LANES), jnp.float32),
            pltpu.VMEM((ROWS, LANES), jnp.float32),
        ],
    )
    return pl.pallas_call(
        functools.partial(unit_kernel, len(queries), merging, chunk),
        grid_spec=grid_spec,
        out_shape=jax.ShapeDtypeStruct((units, node_count, width), wire),
        compiler_params=pltpu.CompilerParams(vmem_limit_bytes=56 * 1024 * 1024),
        cost_estimate=pl.CostEstimate(
            flops=4 * units * node_count * GROUP * block * HD,
            bytes_accessed=units * (4 * block * HD + 4 * node_count * width),
            transcendentals=units * node_count * GROUP * block,
        ),
    )(ids, lens, sizes, base, *operands)


def tree_kernel(first_ref, *refs):
    kv_local = len(refs) - 6
    q_refs = refs[:kv_local]
    k_ref, v_ref, parents_ref, o_ref, l_ref, r_ref = refs[kv_local:]
    rows_owned = q_refs[0].shape[0]
    node_count = k_ref.shape[0]
    steps = (node_count - 1).bit_length()
    node = lax.broadcasted_iota(jnp.int32, (node_count, node_count), 0)
    other = lax.broadcasted_iota(jnp.int32, (node_count, node_count), 1)
    linked = jnp.logical_or(parents_ref[...] == node, node == other)
    reached = linked.astype(jnp.float32)
    for _ in range(steps):
        half = reached.astype(jnp.bfloat16)
        reached = jnp.minimum(jnp.dot(half, half, preferred_element_type=jnp.float32), 1.0)
    r_ref[...] = reached.T
    tile = min(rows_owned, NODES)
    for g in range(kv_local):
        keys = k_ref[:, g * HD : (g + 1) * HD]
        values = v_ref[:, g * HD : (g + 1) * HD]

        @pl.loop(0, rows_owned // tile)
        def _(t):
            start = pl.multiple_of(t * tile, tile)
            first = pl.multiple_of(first_ref[0] + start, tile)
            queries = jnp.concatenate(
                [q_refs[g][pl.ds(start, tile), h * HD : (h + 1) * HD] for h in range(GROUP)], axis=0
            )
            live = jnp.concatenate([r_ref[pl.ds(first, tile), :]] * GROUP, axis=0) > 0.5
            scores = lax.dot_general(
                queries, keys, (((1,), (1,)), ((), ())), preferred_element_type=jnp.float32
            )
            scores = jnp.where(live, scores, negative_fill)
            peaks = jnp.max(scores, axis=1, keepdims=True)
            weights = jnp.where(live, jnp.exp2((scores - peaks) * exp2_scale), 0.0)
            totals = jnp.maximum(jnp.sum(weights, axis=1, keepdims=True), 1.0)
            sums = jnp.dot(weights.astype(jnp.bfloat16), values, preferred_element_type=jnp.float32)
            partials = sums / totals
            for h in range(GROUP):
                o_ref[g, pl.ds(start, tile), h * HD : (h + 1) * HD] = partials[h * tile : (h + 1) * tile, :]
            logs = jnp.broadcast_to(peaks * softmax_scale + jnp.log(totals), (GROUP * tile, LANES))
            l_ref[g, pl.ds(start, tile), :] = place_logs([logs[h * tile : (h + 1) * tile] for h in range(GROUP)])


def tree_attention(queries, keys, values, parents, first):
    rows = queries[0].shape[0]
    node_count = keys.shape[0]
    kv_local = len(queries)
    vmem = pl.BlockSpec(memory_space=pltpu.VMEM)
    return pl.pallas_call(
        tree_kernel,
        in_specs=[pl.BlockSpec(memory_space=pltpu.SMEM)] + [vmem] * (kv_local + 3),
        out_specs=[vmem, vmem],
        out_shape=[
            jax.ShapeDtypeStruct((kv_local, rows, WIDE), jnp.float32),
            jax.ShapeDtypeStruct((kv_local, rows, LANES), jnp.float32),
        ],
        scratch_shapes=[pltpu.VMEM((node_count, node_count), jnp.float32)],
        compiler_params=pltpu.CompilerParams(vmem_limit_bytes=56 * 1024 * 1024),
        cost_estimate=pl.CostEstimate(flops=10**9, bytes_accessed=10**7, transcendentals=10**6),
    )(first, *queries, keys, values, parents)


def merge_kernel(parts, alive_ref, *refs):
    kv_local = len(parts)
    o_ref = refs[-1]
    tree_ref, tree_logs_ref = refs[-3], refs[-2]
    rows = o_ref.shape[0]
    lane = lax.broadcasted_iota(jnp.int32, (LANES, WIDE), 0)
    head = lax.broadcasted_iota(jnp.int32, (LANES, WIDE), 1) // HD
    spread = jnp.logical_and(lane % GROUP == head, lane < 3 * GROUP).astype(jnp.bfloat16)
    group = lax.broadcasted_iota(jnp.int32, (rows, LANES), 1) // GROUP
    at_part = 0
    for g in range(kv_local):
        part_refs = refs[at_part : at_part + parts[g]]
        at_part += parts[g]
        logs = [join_logs(ref[0, :, WIDE:]) for ref in part_refs] + [tree_logs_ref[g]]
        top = functools.reduce(jnp.maximum, logs)
        weights = [jnp.exp(log - top) for log in logs]
        scale = 1.0 / functools.reduce(jnp.add, weights)
        total = None
        for j, weight in enumerate(weights):
            share = jnp.where(group == 0, weight * scale, 0.0)
            share = share + pltpu.roll(share, GROUP, 1) + pltpu.roll(share, 2 * GROUP, 1)
            wide = jnp.dot(split_logs(share), spread, preferred_element_type=jnp.float32)
            piece = tree_ref[g] if j == parts[g] else part_refs[j][0, :, :WIDE].astype(jnp.float32)
            total = wide * piece if total is None else total + wide * piece
        alive = alive_ref[:, :1] > 0.5
        o_ref[:, g * WIDE : (g + 1) * WIDE] = jnp.where(alive, total, 0.0).astype(o_ref.dtype)


def merge(parts, tree_partials, tree_logs, alive):
    kv_local, rows, _ = tree_partials.shape
    tile = min(rows, NODES)
    flat = [pair for of_head in parts for pair in of_head]
    return pl.pallas_call(
        functools.partial(merge_kernel, [len(of_head) for of_head in parts]),
        grid=(rows // tile,),
        in_specs=[pl.BlockSpec((tile, LANES), lambda i: (i, 0))]
        + [
            pl.BlockSpec((1, tile, WIDE + LANES), functools.partial(lambda u, i: (u, i, 0), unit))
            for _, unit in flat
        ]
        + [
            pl.BlockSpec((kv_local, tile, WIDE), lambda i: (0, i, 0)),
            pl.BlockSpec((kv_local, tile, LANES), lambda i: (0, i, 0)),
        ],
        out_specs=pl.BlockSpec((tile, kv_local * WIDE), lambda i: (i, 0)),
        out_shape=jax.ShapeDtypeStruct((rows, kv_local * WIDE), jnp.bfloat16),
        compiler_params=pltpu.CompilerParams(vmem_limit_bytes=48 * 1024 * 1024),
    )(alive, *[array for array, _ in flat], tree_partials, tree_logs)


def exchange(array, distance):
    owners = lax.axis_size("req")
    return lax.ppermute(array, "req", [(r, r ^ distance) for r in range(owners)])


def body(
    queries, cache_keys, cache_values, tree_keys, tree_values, parents, tree_sizes, cache_lens
):
    owner_index = lax.axis_index("req")
    owners = lax.axis_size("req")
    requests = cache_keys.shape[0]
    block = cache_keys.shape[1]
    kv_local = cache_keys.shape[2] // HD
    node_count = parents.shape[1]
    rows_owned = tree_keys.shape[0]
    head_devices = lax.axis_size("head")
    own = []
    for g in range(kv_local):
        columns = [
            queries[:, (d * kv_local + g) * WIDE : (d * kv_local + g + 1) * WIDE] for d in range(head_devices)
        ]
        mine = jnp.concatenate(columns, axis=1) if kv_local > 1 else queries
        own.append(lax.all_to_all(mine, "head", split_axis=1, concat_axis=0, tiled=True))

    first_row = owner_index * rows_owned
    request = first_row // node_count
    first_node = first_row % node_count
    if rows_owned < node_count:
        every_key = lax.all_gather(tree_keys, "req", axis=0, tiled=True)
        every_value = lax.all_gather(tree_values, "req", axis=0, tiled=True)
        own_keys = lax.dynamic_slice_in_dim(every_key, request * node_count, node_count, 0)
        own_values = lax.dynamic_slice_in_dim(every_value, request * node_count, node_count, 0)
    else:
        own_keys, own_values = tree_keys, tree_values
    size = lax.dynamic_index_in_dim(tree_sizes, request, 0, keepdims=False)
    own_parents = lax.dynamic_slice_in_dim(parents, request, 1, 0)

    def attend_tree(after=None):
        first = first_node[None]
        if after is not None:
            first, _ = lax.optimization_barrier((first, after))
        return tree_attention(own, own_keys, own_values, own_parents, first)

    alive = first_node + jnp.arange(rows_owned, dtype=jnp.int32) < size
    alive = jnp.broadcast_to(alive[:, None].astype(jnp.float32), (rows_owned, LANES))
    base = (owner_index * block)[None]

    def attend(queries, targets, blocks, kv_head, received=None, offset=0, after=None):
        ids = jnp.stack([jnp.asarray(i, jnp.int32) for i in [*targets, *blocks, offset]])
        if after is not None:
            ids, _ = lax.optimization_barrier((ids, after))
        return unit_attention(
            queries, ids, kv_head, cache_keys, cache_values, cache_lens, tree_sizes, base, node_count, received
        )

    if owners == 8 and rows_owned == node_count and kv_local == 2:
        r = owner_index
        core = r % 2
        cores = [[2 * i, 2 * i + 1] for i in range(4)]
        ours, theirs = [r ^ 2, r ^ 4, r ^ 6], [r ^ 3, r ^ 5, r ^ 7]

        def swap(partials):
            return lax.all_gather(partials, "req", axis=0, tiled=True, axis_index_groups=cores)

        def send(partials):
            return [exchange(partials[i : i + 1], 2 * (i + 1) + 1) for i in range(3)]

        first = lax.all_gather(own[0], "req", axis=0, tiled=True)
        near0 = attend([own[0], exchange(own[0], 1)], [r, r ^ 1], [0, 0], 0)
        late, _ = lax.optimization_barrier((own[1], near0))
        second = lax.all_gather(late, "req", axis=0, tiled=True)
        from_near0 = exchange(near0[1:2], 1)
        tree_partials, tree_logs = attend_tree(near0)
        ours0 = attend(first, ours, ours, 0, after=(tree_logs, from_near0))
        swapped0 = swap(ours0)
        ours1 = attend(second, ours, ours, 1, after=ours0)
        swapped1 = swap(ours1)
        sibling_part = 3 * (1 - core)
        theirs0 = attend(first, theirs, theirs, 0, swapped0, sibling_part, after=ours1)
        sent0 = send(theirs0)
        theirs1 = attend(second, theirs, theirs, 1, swapped1, sibling_part, after=theirs0)
        sent1 = send(theirs1)
        near1 = attend(second, [r, r ^ 1], [r, r ^ 1], 1, after=(theirs1, sent0))
        from_near1 = exchange(near1[1:2], 1)
        parts = [
            [(near0, 0), (from_near0, 0)] + [(piece, 0) for piece in sent0],
            [(near1, 0), (from_near1, 0)] + [(piece, 0) for piece in sent1],
        ]
        return merge(parts, tree_partials, tree_logs, alive)

    tree_partials, tree_logs = attend_tree()
    every = [lax.all_gather(q, "req", axis=0, tiled=True) for q in own]
    targets = list(range(requests))
    partials = jnp.stack([attend(every[g], targets, targets, g) for g in range(kv_local)])
    partials = partials.reshape(kv_local, owners, rows_owned, WIDE + LANES)
    partials = lax.all_to_all(partials, "req", split_axis=1, concat_axis=1)
    partials = partials.reshape(kv_local * owners, rows_owned, WIDE + LANES)
    parts = [[(partials, g * owners + j) for j in range(owners)] for g in range(kv_local)]
    return merge(parts, tree_partials, tree_logs, alive)


def solution(mesh):
    placed = (
        P(("req", "head"), None),
        P(None, "req", "head"),
        P(None, "req", "head"),
        P("req", "head"),
        P("req", "head"),
        P(),
        P(),
        P(),
    )
    return jax.shard_map(
        body, mesh=mesh, in_specs=placed, out_specs=P("req", "head"), check_vma=False
    )
```

```python
import functools
import math

import jax
import jax.numpy as jnp
from jax import lax
from jax.experimental import pallas as pl
from jax.experimental.pallas import tpu as pltpu
from jax.sharding import PartitionSpec as P

NH = 128
KVH = 8
HD = 128
GROUP = NH // KVH
WIDE = GROUP * HD
LANES = 128
NODES = 32
ROWS = GROUP * NODES

negative_fill = -1e30
softmax_scale = 1.0 / math.sqrt(HD)
exp2_scale = softmax_scale * math.log2(math.e)
wire = jnp.bfloat16


def lane_max(scores):
    best = scores[:, :LANES]
    for at in range(LANES, scores.shape[1], LANES):
        best = jnp.maximum(best, scores[:, at : at + LANES])
    return best


def place_logs(logs):
    lane = lax.broadcasted_iota(jnp.int32, logs[0].shape, 1) % GROUP
    placed = logs[0]
    for head in range(1, GROUP):
        placed = jnp.where(lane == head, logs[head], placed)
    return placed


def split_logs(logs):
    high = logs.astype(wire).astype(jnp.float32)
    rest = logs - high
    middle = rest.astype(wire).astype(jnp.float32)
    group = lax.broadcasted_iota(jnp.int32, logs.shape, 1) // GROUP
    parts = jnp.where(group == 0, high, jnp.where(group == 1, middle, rest - middle))
    return parts.astype(wire)


def join_logs(parts):
    parts = parts.astype(jnp.float32)
    return parts + pltpu.roll(parts, LANES - GROUP, 1) + pltpu.roll(parts, LANES - 2 * GROUP, 1)


def unit_kernel(listed, merging, split, chunk, ids_ref, lens_ref, sizes_ref, base_ref, *refs):
    q_refs, refs = refs[:listed], refs[listed:]
    k_ref, v_ref, refs = refs[0], refs[1], refs[2:]
    r_ref, refs = (refs[0], refs[1:]) if merging else (None, refs)
    out_refs, refs = refs[:split], refs[split:]
    o_ref, q_ref, p_ref, x_ref, a_ref, f_ref, t_ref, h_ref, g_ref, m_ref = refs
    unit = pl.program_id(0)
    request = ids_ref[unit]
    block = k_ref.shape[1]
    node_count = q_ref.shape[0]
    live = jnp.clip(lens_ref[request] - base_ref[0], 0, block)
    tiles = (sizes_ref[request] + NODES - 1) // NODES
    step = 256
    part = min(block, 512)
    part_chunks = (live + part - 1) // part
    whole_chunks = live // chunk

    def score(queries, at, width):
        return lax.dot_general(
            queries,
            k_ref[0, pl.ds(at, width), :],
            (((1,), (1,)), ((), ())),
            preferred_element_type=jnp.float32,
        )

    def weigh(scores):
        return [
            jnp.exp2(scores[:, i : i + LANES] * exp2_scale - h_ref[...]).astype(jnp.bfloat16)
            for i in range(0, scores.shape[1], LANES)
        ]

    def masked(scores, at):
        column = lax.broadcasted_iota(jnp.int32, scores.shape, 1)
        return jnp.where(column < live - at, scores, negative_fill)

    def shift_of(best):
        peaks = jnp.max(best, axis=1, keepdims=True) * exp2_scale
        return jnp.broadcast_to(peaks, best.shape)

    def take(t):
        start = pl.multiple_of(t * NODES, NODES)
        return jnp.concatenate(
            [q_ref[pl.ds(start, NODES), h * HD : (h + 1) * HD] for h in range(GROUP)], axis=0
        )

    def sample(t):
        queries = take(t)
        return queries, shift_of(masked(score(queries, 0, LANES), 0))

    def chunk_sums(at, place):
        for i in range(0, chunk, step):
            for j, piece in enumerate(weigh(score(t_ref[...], at + i, step))):
                p_ref[:, place + i + j * LANES : place + i + (j + 1) * LANES] = piece
        return jnp.dot(
            p_ref[:, place : place + chunk], x_ref[pl.ds(at, chunk), :], preferred_element_type=jnp.float32
        )

    def whole_block():
        chunks = block // chunk
        for c in range(chunks):
            sums = chunk_sums(c * chunk, c * chunk)
            if c > 0:
                sums = a_ref[...] + sums
            if c < chunks - 1:
                a_ref[...] = sums
            else:
                f_ref[...] = sums

    def part_block():
        f_ref[...] = jnp.zeros(f_ref.shape, jnp.float32)

        @pl.loop(0, whole_chunks)
        def _(c):
            f_ref[...] += chunk_sums(pl.multiple_of(c * chunk, chunk), 0)

        @pl.loop(whole_chunks * (chunk // part), part_chunks)
        def _(c):
            at = pl.multiple_of(c * part, part)
            weights = jnp.concatenate(weigh(masked(score(t_ref[...], at, part), at)), axis=1)
            f_ref[...] += jnp.dot(weights, x_ref[pl.ds(at, part), :], preferred_element_type=jnp.float32)

    def exact_shift():
        g_ref[...] = jnp.full(g_ref.shape, negative_fill, jnp.float32)

        @pl.loop(0, part_chunks)
        def _(c):
            at = pl.multiple_of(c * part, part)
            best = lane_max(masked(score(t_ref[...], at, part), at))
            g_ref[...] = jnp.maximum(g_ref[...], best)

        h_ref[...] = shift_of(g_ref[...])

    def finish(t):
        rows = pl.ds(pl.multiple_of(jnp.maximum(t, 0) * NODES, NODES), NODES)
        totals = f_ref[:, LANES:]
        m_ref[...] = jnp.maximum(m_ref[...], jnp.where(t >= 0, totals, 0.0))
        inverse = 1.0 / totals
        logs = g_ref[...] * math.log(2.0) + jnp.log(totals)
        other_logs = join_logs(r_ref[0, rows, WIDE:]) if merging else None
        head_logs = []
        for h in range(GROUP):
            at = slice(h * NODES, (h + 1) * NODES)
            columns = slice(h * HD, (h + 1) * HD)
            partial = f_ref[at, :LANES] * inverse[at]
            log = logs[at]
            if merging:
                other = jnp.broadcast_to(other_logs[:, h : h + 1], (NODES, LANES))
                top = jnp.maximum(log, other)
                own_weight = jnp.exp(log - top)
                other_weight = jnp.exp(other - top)
                total = own_weight + other_weight
                mixed = partial * own_weight + r_ref[0, rows, columns].astype(jnp.float32) * other_weight
                partial = mixed / total
                log = top + jnp.log(total)
            o_ref[0, rows, columns] = partial.astype(wire)
            head_logs.append(log)
        o_ref[0, rows, WIDE:] = split_logs(place_logs(head_logs))

    @pl.when(unit == 0)
    def _():
        x_ref[:, HD:] = jnp.ones((block, LANES), x_ref.dtype)

    @pl.when(live == 0)
    def _():
        if merging:
            o_ref[...] = r_ref[...]
        else:
            o_ref[0, :, :WIDE] = jnp.zeros((node_count, WIDE), wire)
            o_ref[0, :, WIDE:] = split_logs(jnp.full((node_count, LANES), negative_fill, jnp.float32))

    @pl.when(live > 0)
    def _():
        if listed == 1:
            q_ref[...] = q_refs[0][...]
        else:
            for i in range(listed):

                @pl.when(unit == i)
                def _():
                    q_ref[...] = q_refs[i][...]

        x_ref[:, :HD] = v_ref[0]
        m_ref[...] = jnp.zeros(m_ref.shape, jnp.float32)

    @pl.when(live == block)
    def _():
        queries, shift = sample(0)
        t_ref[...] = queries
        h_ref[...] = shift

        @pl.loop(0, tiles)
        def _(t):
            finish(t - 1)
            g_ref[...] = h_ref[...]
            queries, shift = sample(jnp.minimum(t + 1, tiles - 1))
            whole_block()
            t_ref[...] = queries
            h_ref[...] = shift

        finish(tiles - 1)

    @pl.loop(0, 2)
    def _(exact):
        overflowed = jnp.logical_not(jnp.max(m_ref[...]) < 2.0**100)
        first = jnp.logical_and(exact == 0, live < block)
        again = jnp.logical_and(exact == 1, overflowed)

        @pl.when(jnp.logical_and(live > 0, jnp.logical_or(first, again)))
        def _():
            @pl.loop(0, tiles)
            def _(t):
                t_ref[...] = take(t)

                @pl.when(exact == 0)
                def _():
                    h_ref[...] = shift_of(masked(score(t_ref[...], 0, LANES), 0))

                @pl.when(exact == 1)
                def _():
                    exact_shift()

                part_block()
                g_ref[...] = h_ref[...]
                finish(t)

    for i in range(split):

        @pl.when(unit == i)
        def _():
            out_refs[i][...] = o_ref[...]


def unit_attention(queries, ids, kv_head, cache_keys, cache_values, lens, sizes, base, node_count, received=None, split=False):
    units = ids.shape[0] // 2
    block = cache_keys.shape[1]
    chunk = min(block, 1024)
    merging = received is not None
    width = WIDE + LANES

    def cache_map(u, ids_ref, *_):
        return (ids_ref[u], 0, kv_head)

    def unit_map(u, *_):
        return (u, 0, 0)

    def received_map(u, ids_ref, *_):
        return (ids_ref[2 * units] + u, 0, 0)

    if isinstance(queries, list):
        in_specs = [
            pl.BlockSpec((node_count, WIDE), functools.partial(lambda i, u, ids_ref, *_: (ids_ref[units + i], 0), i))
            for i in range(units)
        ]
    else:
        queries = [queries]
        in_specs = [pl.BlockSpec((node_count, WIDE), lambda u, ids_ref, *_: (ids_ref[units + u], 0))]
    operands = queries + [cache_keys, cache_values]
    in_specs = in_specs + [pl.BlockSpec((1, block, HD), cache_map)] * 2
    if merging:
        in_specs.append(pl.BlockSpec((1, node_count, width), received_map))
        operands.append(received)
    out_specs = pl.BlockSpec((1, node_count, width), unit_map)
    out_shape = jax.ShapeDtypeStruct((units, node_count, width), wire)
    held = []
    if split:
        out_specs = [pl.BlockSpec((1, node_count, width), lambda u, *_: (0, 0, 0))] * units
        out_shape = [jax.ShapeDtypeStruct((1, node_count, width), wire)] * units
        held = [pltpu.VMEM((1, node_count, width), wire)]
    grid_spec = pltpu.PrefetchScalarGridSpec(
        num_scalar_prefetch=4,
        grid=(units,),
        in_specs=in_specs,
        out_specs=out_specs,
        scratch_shapes=held
        + [
            pltpu.VMEM((node_count, WIDE), jnp.bfloat16),
            pltpu.VMEM((ROWS, block), jnp.bfloat16),
            pltpu.VMEM((block, 2 * LANES), jnp.bfloat16),
            pltpu.VMEM((ROWS, 2 * LANES), jnp.float32),
            pltpu.VMEM((ROWS, 2 * LANES), jnp.float32),
            pltpu.VMEM((ROWS, HD), jnp.bfloat16),
            pltpu.VMEM((ROWS, LANES), jnp.float32),
            pltpu.VMEM((ROWS, LANES), jnp.float32),
            pltpu.VMEM((ROWS, LANES), jnp.float32),
        ],
    )
    return pl.pallas_call(
        functools.partial(unit_kernel, len(queries), merging, units if split else 0, chunk),
        grid_spec=grid_spec,
        out_shape=out_shape,
        compiler_params=pltpu.CompilerParams(vmem_limit_bytes=56 * 1024 * 1024),
        cost_estimate=pl.CostEstimate(
            flops=4 * units * node_count * GROUP * block * HD,
            bytes_accessed=units * (4 * block * HD + 4 * node_count * width),
            transcendentals=units * node_count * GROUP * block,
        ),
    )(ids, lens, sizes, base, *operands)


def tree_kernel(first_ref, *refs):
    kv_local = len(refs) - 6
    q_refs = refs[:kv_local]
    k_ref, v_ref, parents_ref, o_ref, l_ref, r_ref = refs[kv_local:]
    rows_owned = q_refs[0].shape[0]
    node_count = k_ref.shape[0]
    steps = (node_count - 1).bit_length()
    node = lax.broadcasted_iota(jnp.int32, (node_count, node_count), 0)
    other = lax.broadcasted_iota(jnp.int32, (node_count, node_count), 1)
    linked = jnp.logical_or(parents_ref[...] == node, node == other)
    reached = linked.astype(jnp.float32)
    for _ in range(steps):
        half = reached.astype(jnp.bfloat16)
        reached = jnp.minimum(jnp.dot(half, half, preferred_element_type=jnp.float32), 1.0)
    r_ref[...] = reached.T
    tile = min(rows_owned, NODES)
    for g in range(kv_local):
        keys = k_ref[:, g * HD : (g + 1) * HD]
        values = v_ref[:, g * HD : (g + 1) * HD]

        @pl.loop(0, rows_owned // tile)
        def _(t):
            start = pl.multiple_of(t * tile, tile)
            first = pl.multiple_of(first_ref[0] + start, tile)
            queries = jnp.concatenate(
                [q_refs[g][pl.ds(start, tile), h * HD : (h + 1) * HD] for h in range(GROUP)], axis=0
            )
            live = jnp.concatenate([r_ref[pl.ds(first, tile), :]] * GROUP, axis=0) > 0.5
            scores = lax.dot_general(
                queries, keys, (((1,), (1,)), ((), ())), preferred_element_type=jnp.float32
            )
            scores = jnp.where(live, scores, negative_fill)
            peaks = jnp.max(scores, axis=1, keepdims=True)
            weights = jnp.where(live, jnp.exp2((scores - peaks) * exp2_scale), 0.0)
            totals = jnp.maximum(jnp.sum(weights, axis=1, keepdims=True), 1.0)
            sums = jnp.dot(weights.astype(jnp.bfloat16), values, preferred_element_type=jnp.float32)
            partials = sums / totals
            for h in range(GROUP):
                o_ref[g, pl.ds(start, tile), h * HD : (h + 1) * HD] = partials[h * tile : (h + 1) * tile, :]
            logs = jnp.broadcast_to(peaks * softmax_scale + jnp.log(totals), (GROUP * tile, LANES))
            l_ref[g, pl.ds(start, tile), :] = place_logs([logs[h * tile : (h + 1) * tile] for h in range(GROUP)])


def tree_attention(queries, keys, values, parents, first):
    rows = queries[0].shape[0]
    node_count = keys.shape[0]
    kv_local = len(queries)
    vmem = pl.BlockSpec(memory_space=pltpu.VMEM)
    return pl.pallas_call(
        tree_kernel,
        in_specs=[pl.BlockSpec(memory_space=pltpu.SMEM)] + [vmem] * (kv_local + 3),
        out_specs=[vmem, vmem],
        out_shape=[
            jax.ShapeDtypeStruct((kv_local, rows, WIDE), jnp.float32),
            jax.ShapeDtypeStruct((kv_local, rows, LANES), jnp.float32),
        ],
        scratch_shapes=[pltpu.VMEM((node_count, node_count), jnp.float32)],
        compiler_params=pltpu.CompilerParams(vmem_limit_bytes=56 * 1024 * 1024),
        cost_estimate=pl.CostEstimate(flops=10**9, bytes_accessed=10**7, transcendentals=10**6),
    )(first, *queries, keys, values, parents)


def merge_kernel(parts, alive_ref, *refs):
    kv_local = len(parts)
    o_ref = refs[-1]
    tree_ref, tree_logs_ref = refs[-3], refs[-2]
    rows = o_ref.shape[0]
    lane = lax.broadcasted_iota(jnp.int32, (LANES, WIDE), 0)
    head = lax.broadcasted_iota(jnp.int32, (LANES, WIDE), 1) // HD
    spread = jnp.logical_and(lane % GROUP == head, lane < 3 * GROUP).astype(jnp.bfloat16)
    group = lax.broadcasted_iota(jnp.int32, (rows, LANES), 1) // GROUP
    at_part = 0
    for g in range(kv_local):
        part_refs = refs[at_part : at_part + parts[g]]
        at_part += parts[g]
        logs = [join_logs(ref[0, :, WIDE:]) for ref in part_refs] + [tree_logs_ref[g]]
        top = functools.reduce(jnp.maximum, logs)
        weights = [jnp.exp(log - top) for log in logs]
        scale = 1.0 / functools.reduce(jnp.add, weights)
        total = None
        for j, weight in enumerate(weights):
            share = jnp.where(group == 0, weight * scale, 0.0)
            share = share + pltpu.roll(share, GROUP, 1) + pltpu.roll(share, 2 * GROUP, 1)
            wide = jnp.dot(split_logs(share), spread, preferred_element_type=jnp.float32)
            piece = tree_ref[g] if j == parts[g] else part_refs[j][0, :, :WIDE].astype(jnp.float32)
            total = wide * piece if total is None else total + wide * piece
        alive = alive_ref[:, :1] > 0.5
        o_ref[:, g * WIDE : (g + 1) * WIDE] = jnp.where(alive, total, 0.0).astype(o_ref.dtype)


def merge(parts, tree_partials, tree_logs, alive):
    kv_local, rows, _ = tree_partials.shape
    tile = min(rows, NODES)
    flat = [pair for of_head in parts for pair in of_head]
    return pl.pallas_call(
        functools.partial(merge_kernel, [len(of_head) for of_head in parts]),
        grid=(rows // tile,),
        in_specs=[pl.BlockSpec((tile, LANES), lambda i: (i, 0))]
        + [
            pl.BlockSpec((1, tile, WIDE + LANES), functools.partial(lambda u, i: (u, i, 0), unit))
            for _, unit in flat
        ]
        + [
            pl.BlockSpec((kv_local, tile, WIDE), lambda i: (0, i, 0)),
            pl.BlockSpec((kv_local, tile, LANES), lambda i: (0, i, 0)),
        ],
        out_specs=pl.BlockSpec((tile, kv_local * WIDE), lambda i: (i, 0)),
        out_shape=jax.ShapeDtypeStruct((rows, kv_local * WIDE), jnp.bfloat16),
        compiler_params=pltpu.CompilerParams(vmem_limit_bytes=48 * 1024 * 1024),
    )(alive, *[array for array, _ in flat], tree_partials, tree_logs)


def exchange(array, distance):
    owners = lax.axis_size("req")
    return lax.ppermute(array, "req", [(r, r ^ distance) for r in range(owners)])


def body(
    queries, cache_keys, cache_values, tree_keys, tree_values, parents, tree_sizes, cache_lens
):
    owner_index = lax.axis_index("req")
    owners = lax.axis_size("req")
    requests = cache_keys.shape[0]
    block = cache_keys.shape[1]
    kv_local = cache_keys.shape[2] // HD
    node_count = parents.shape[1]
    rows_owned = tree_keys.shape[0]
    head_devices = lax.axis_size("head")
    own = []
    for g in range(kv_local):
        columns = [
            queries[:, (d * kv_local + g) * WIDE : (d * kv_local + g + 1) * WIDE] for d in range(head_devices)
        ]
        mine = jnp.concatenate(columns, axis=1) if kv_local > 1 else queries
        own.append(lax.all_to_all(mine, "head", split_axis=1, concat_axis=0, tiled=True))

    first_row = owner_index * rows_owned
    request = first_row // node_count
    first_node = first_row % node_count
    if rows_owned < node_count:
        every_key = lax.all_gather(tree_keys, "req", axis=0, tiled=True)
        every_value = lax.all_gather(tree_values, "req", axis=0, tiled=True)
        own_keys = lax.dynamic_slice_in_dim(every_key, request * node_count, node_count, 0)
        own_values = lax.dynamic_slice_in_dim(every_value, request * node_count, node_count, 0)
    else:
        own_keys, own_values = tree_keys, tree_values
    size = lax.dynamic_index_in_dim(tree_sizes, request, 0, keepdims=False)
    own_parents = lax.dynamic_slice_in_dim(parents, request, 1, 0)

    def attend_tree(after=None):
        first = first_node[None]
        if after is not None:
            first, _ = lax.optimization_barrier((first, after))
        return tree_attention(own, own_keys, own_values, own_parents, first)

    alive = first_node + jnp.arange(rows_owned, dtype=jnp.int32) < size
    alive = jnp.broadcast_to(alive[:, None].astype(jnp.float32), (rows_owned, LANES))
    base = (owner_index * block)[None]

    def attend(queries, targets, blocks, kv_head, received=None, offset=0, after=None, split=False):
        ids = jnp.stack([jnp.asarray(i, jnp.int32) for i in [*targets, *blocks, offset]])
        if after is not None:
            ids, _ = lax.optimization_barrier((ids, after))
        return unit_attention(
            queries, ids, kv_head, cache_keys, cache_values, cache_lens, tree_sizes, base, node_count, received, split
        )

    if owners == 8 and rows_owned == node_count and kv_local == 2:
        r = owner_index
        core = r % 2
        cores = [[2 * i, 2 * i + 1] for i in range(4)]
        ours, theirs = [r ^ 2, r ^ 4, r ^ 6], [r ^ 3, r ^ 5, r ^ 7]

        def swap(partials):
            return lax.all_gather(partials, "req", axis=0, tiled=True, axis_index_groups=cores)

        def send(partials):
            return [exchange(partials[i], 2 * (i + 1) + 1) for i in range(3)]

        first = lax.all_gather(own[0], "req", axis=0, tiled=True)
        near0 = attend([own[0], exchange(own[0], 1)], [r, r ^ 1], [0, 0], 0, split=True)
        late, _ = lax.optimization_barrier((own[1], near0))
        second = lax.all_gather(late, "req", axis=0, tiled=True)
        from_near0 = exchange(near0[1], 1)
        tree_partials, tree_logs = attend_tree(near0)
        ours0 = attend(first, ours, ours, 0, after=(tree_logs, from_near0))
        swapped0 = swap(ours0)
        ours1 = attend(second, ours, ours, 1, after=ours0)
        swapped1 = swap(ours1)
        sibling_part = 3 * (1 - core)
        theirs0 = attend(first, theirs, theirs, 0, swapped0, sibling_part, after=ours1, split=True)
        sent0 = send(theirs0)
        theirs1 = attend(second, theirs, theirs, 1, swapped1, sibling_part, after=theirs0, split=True)
        sent1 = send(theirs1)
        near1 = attend(second, [r, r ^ 1], [r, r ^ 1], 1, after=(theirs1, sent0), split=True)
        from_near1 = exchange(near1[1], 1)
        parts = [
            [(near0[0], 0), (from_near0, 0)] + [(piece, 0) for piece in sent0],
            [(near1[0], 0), (from_near1, 0)] + [(piece, 0) for piece in sent1],
        ]
        return merge(parts, tree_partials, tree_logs, alive)

    tree_partials, tree_logs = attend_tree()
    every = [lax.all_gather(q, "req", axis=0, tiled=True) for q in own]
    targets = list(range(requests))
    partials = jnp.stack([attend(every[g], targets, targets, g) for g in range(kv_local)])
    partials = partials.reshape(kv_local, owners, rows_owned, WIDE + LANES)
    partials = lax.all_to_all(partials, "req", split_axis=1, concat_axis=1)
    partials = partials.reshape(kv_local * owners, rows_owned, WIDE + LANES)
    parts = [[(partials, g * owners + j) for j in range(owners)] for g in range(kv_local)]
    return merge(parts, tree_partials, tree_logs, alive)


def solution(mesh):
    placed = (
        P(("req", "head"), None),
        P(None, "req", "head"),
        P(None, "req", "head"),
        P("req", "head"),
        P("req", "head"),
        P(),
        P(),
        P(),
    )
    return jax.shard_map(
        body, mesh=mesh, in_specs=placed, out_specs=P("req", "head"), check_vma=False
    )
```
